128 devices in a mesh: blk: 16 (over x_hi, z, core), rep: 8 (over y, x_lo).
Axes of the slice: x: 4 (x_hi: 2, x_lo: 2; x = x_hi * 2 + x_lo), y: 4, z: 4, core: 2. Of those that a mesh axis runs over, the one named last changes fastest.
Arguments:
- features: bfloat16 [65536, 128], P(('blk', 'rep')), may hold values from -6 to 6
- cotangent: bfloat16 [65536, 128], P(('blk', 'rep')), may hold values from -6 to 6
- w_self: bfloat16 [128, 128], replicated, may hold values from -0.5 to 0.5
- w_neigh: bfloat16 [128, 128], replicated, may hold values from -0.5 to 0.5
- out_bias: float32 [128], replicated, may hold values from -3 to 3
- tile_values: bfloat16 [16, 8, 16, 32, 128, 128], P('blk', 'rep'), may hold values from 0 to 12, as said below
- dest_tile: int32 [16, 8, 16, 32], P('blk', 'rep'), may hold values from 0 to 31
- src_tile: int32 [16, 8, 16, 32], P('blk', 'rep'), may hold values from 0 to 3
- tile_count: int32 [16, 8, 16], P('blk', 'rep'), may hold values from 0 to 32, as said below
Outputs:
- activated: bfloat16 [65536, 128], P(('blk', 'rep'))
- grad_features: float32 [65536, 128], P(('blk', 'rep'))
- grad_w_self: float32 [128, 128], replicated
- grad_w_neigh: float32 [128, 128], replicated
- grad_bias: float32 [128], replicated
The draws below stay inside these ranges and needn't reach their ends.
Inputs may be any that keep to these rules, and one draw needn't show every extreme that they name: `tile_values`: every entry is positive. `tile_count`: for every destination partition and member, the count for the source partition equal to the destination partition is 32.
All inputs are finite; a program needn't handle non-finite values.
Results may differ from the reference program's by a relative error of at most 0.007.
Values may be sent and summed in bfloat16 or wider, within the bound.
No kernel may reach another device: no remote copies, remote signals or barrier semaphores. Data moves between devices by JAX's collectives and lax.ppermute only.
A program may use at most 128 MiB of HBM per device.

```python
import jax
import jax.numpy as jnp
from jax import lax

F = 128
TILE = 128
NODE_DEV = 512
SLOTS = 32
NODES = 65536
N_BLK = 16
N_REP = 8


def draw_tile_values(key, part):
    key = jax.random.fold_in(key, 11)
    first, second, third = jax.random.split(key, 3)
    shape = (N_BLK, N_REP, N_BLK, SLOTS, TILE, TILE)
    base = jax.random.uniform(first, shape, jnp.float32, 0.05, 1.0)
    spread = 1.0
    rows = jnp.exp(jax.random.uniform(second, shape[:-1] + (1,), jnp.float32, -spread, spread))
    cols = jnp.exp(jax.random.uniform(third, shape[:-2] + (1, TILE), jnp.float32, -spread, spread))
    return (base * rows * cols).astype(jnp.bfloat16)


def draw_tile_count(key, part):
    key = jax.random.fold_in(key, 12)
    counts = jax.random.randint(key, (N_BLK, N_REP, N_BLK), 0, SLOTS + 1, jnp.int32)
    own = jnp.arange(N_BLK, dtype=jnp.int32)[:, None, None] == jnp.arange(N_BLK, dtype=jnp.int32)[None, None, :]
    return jnp.where(own, jnp.int32(SLOTS), counts)


def set_ends(entries, stream_key, least, high):
    shape = entries.shape
    place = [jax.random.randint(jax.random.fold_in(stream_key, axis), (), 0, shape[axis]) for axis in range(len(shape))]
    entries = entries.at[tuple(place)].set(least)
    longest = shape.index(max(shape))
    place[longest] = (place[longest] + 1) % shape[longest]
    return entries.at[tuple(place)].set(high)


def block_scale(rng, dims, cuts, least, high):
    loudness = 1.0
    for position, blocks in cuts:
        heights = jax.random.uniform(jax.random.fold_in(jax.random.fold_in(rng, 6), position), (blocks,), jnp.float32, least / len(cuts), high / len(cuts))
        loudness = loudness * jnp.repeat(jnp.exp(heights), dims[position] // blocks).reshape((-1,) + (1,) * (len(dims) - 1 - position))
    return loudness


def normal_values(rng, shape, deviation, limit, shards=(), kind=jnp.bfloat16):
    entries = deviation * jax.random.normal(rng, shape, jnp.float32)
    if shards:
        entries = entries * block_scale(rng, shape, shards, -0.22, 0.18)
    return jnp.clip(entries, -limit, limit).astype(kind)


def setup_inputs(seed: int = 0) -> dict:
    seeds = jax.random.split(jax.random.key(seed), 10)
    features = normal_values(seeds[0], (NODES, F), 1.0, 6.0, ((0, 128),))
    cotangent = normal_values(seeds[1], (NODES, F), 1.0, 6.0, ((0, 128),))
    w_self = normal_values(seeds[2], (F, F), F ** -0.5, 0.5)
    w_neigh = normal_values(seeds[3], (F, F), F ** -0.5, 0.5)
    out_bias = normal_values(seeds[4], (F,), 0.5, 3.0, (), jnp.float32)
    tile_values = draw_tile_values(jax.random.fold_in(seeds[9], 71), 0)
    dest_tile = set_ends(jax.random.randint(seeds[6], (N_BLK, N_REP, N_BLK, SLOTS), 0, N_REP * NODE_DEV // TILE), jax.random.fold_in(seeds[6], 1), 0, (N_REP * NODE_DEV // TILE) - 1).astype(jnp.int32)
    src_tile = set_ends(jax.random.randint(seeds[7], (N_BLK, N_REP, N_BLK, SLOTS), 0, NODE_DEV // TILE), jax.random.fold_in(seeds[7], 1), 0, (NODE_DEV // TILE) - 1).astype(jnp.int32)
    tile_count = draw_tile_count(jax.random.fold_in(seeds[9], 71), 0)
    return {"features": features, "cotangent": cotangent, "w_self": w_self, "w_neigh": w_neigh, "out_bias": out_bias, "tile_values": tile_values, "dest_tile": dest_tile, "src_tile": src_tile, "tile_count": tile_count}


def reference(features, cotangent, w_self, w_neigh, out_bias, tile_values, dest_tile, src_tile, tile_count):
    col_tiles = NODE_DEV // TILE
    dest_tiles = N_REP * col_tiles
    members = jnp.arange(N_REP, dtype=jnp.int32)
    parts = jnp.arange(N_BLK, dtype=jnp.int32)
    live = (jnp.arange(SLOTS, dtype=jnp.int32)[None, None, None, :] < tile_count[..., None]).astype(jnp.float32)
    dest_hot = (dest_tile[..., None] == jnp.arange(dest_tiles, dtype=jnp.int32)).astype(jnp.float32) * live[..., None]
    src_hot = (src_tile[..., None] == jnp.arange(col_tiles, dtype=jnp.int32)).astype(jnp.float32) * live[..., None]
    blocks = features.reshape(N_BLK, N_REP, col_tiles, TILE, F)
    high = lax.Precision.HIGHEST

    def forward(carry, source):
        sums, degs = carry
        values = tile_values[:, :, source].astype(jnp.float32)
        picked = blocks[source][members[None, :, None], src_tile[:, :, source]].astype(jnp.float32)
        products = jnp.einsum('brknm,brkmf->brknf', values, picked, precision=high)
        onehot = dest_hot[:, :, source]
        sums = sums + jnp.einsum('brkd,brknf->bdnf', onehot, products, precision=high)
        degs = degs + jnp.einsum('brkd,brkn->bdn', onehot, lax.optimization_barrier(jnp.sum(values, axis=-1)), precision=high)
        return ((sums, degs), None)
    start = (jnp.zeros((N_BLK, dest_tiles, TILE, F), jnp.float32), jnp.zeros((N_BLK, dest_tiles, TILE), jnp.float32))
    (sums, degs), unused = lax.scan(forward, start, parts)
    neighbour_sum = sums.reshape(NODES, F)
    degree = degs.reshape(NODES)
    scale = lax.rsqrt(1.0 + degree)[:, None]
    neighbour_mean = (neighbour_sum * scale).astype(jnp.bfloat16)
    pre = jnp.dot(features, w_self, preferred_element_type=jnp.float32) + jnp.dot(neighbour_mean, w_neigh, preferred_element_type=jnp.float32) + out_bias
    activated = jax.nn.silu(pre).astype(jnp.bfloat16)
    sig = jax.nn.sigmoid(pre)
    grad_pre = (cotangent.astype(jnp.float32) * sig * (1.0 + pre * (1.0 - sig))).astype(jnp.bfloat16)
    grad_w_self = jnp.dot(features.T, grad_pre, preferred_element_type=jnp.float32)
    grad_w_neigh = jnp.dot(neighbour_mean.T, grad_pre, preferred_element_type=jnp.float32)
    grad_bias = lax.optimization_barrier(jnp.sum(grad_pre.astype(jnp.float32), axis=0))
    sum_grad = (jnp.dot(grad_pre, w_neigh.T, preferred_element_type=jnp.float32) * scale).astype(jnp.bfloat16)
    spread = sum_grad.reshape(N_BLK, dest_tiles, TILE, F)

    def backward(carry, source):
        values = tile_values[:, :, source].astype(jnp.float32)
        picked = spread[parts[:, None, None], dest_tile[:, :, source]].astype(jnp.float32)
        products = jnp.einsum('brknm,brknf->brkmf', values, picked, precision=high)
        result = jnp.einsum('brkc,brkmf->rcmf', src_hot[:, :, source], products, precision=high)
        return (carry, result)
    unused, pieces = lax.scan(backward, jnp.zeros((), jnp.float32), parts)
    grad_features = jnp.dot(grad_pre, w_self.T, preferred_element_type=jnp.float32) + pieces.reshape(NODES, F)
    return (activated, grad_features, grad_w_self, grad_w_neigh, grad_bias)
```

```python
import functools

import jax
import jax.numpy as jnp
from jax import lax
from jax.experimental import pallas as pl
from jax.experimental.pallas import tpu as pltpu
from jax.sharding import PartitionSpec as P

f32, bf16 = jnp.float32, jnp.bfloat16
T = 128
SLOTS = 32
NSRC = 4
NDST = 32
REP = 8
CH = 8
U = 4
DEG = 16
WROWS = 40
WX = 2 * WROWS
SMEM = pl.BlockSpec(memory_space=pltpu.SMEM)
VMEM = pl.BlockSpec(memory_space=pltpu.VMEM)
ANY = pl.BlockSpec(memory_space=pl.ANY)


def params(mib=40):
    return pltpu.CompilerParams(vmem_limit_bytes=mib * 1024 * 1024)


def blk_at(dx, dz, dc):
    here = lax.axis_index("blk")
    x, z, c = here // 8, (here // 2) % 4, here % 2
    return (x + dx) % 2 * 8 + (z + dz) % 4 * 2 + (c + dc) % 2


def moved(value, dx, dz, dc):
    pairs = []
    for i in range(16):
        x, z, c = i // 8, (i // 2) % 4, i % 2
        pairs.append((i, (x + dx) % 2 * 8 + (z + dz) % 4 * 2 + (c + dc) % 2))
    return lax.ppermute(value, "blk", pairs)


def high_low(v):
    high = v.astype(bf16)
    return high, (v - high.astype(f32)).astype(bf16)


def start_copies(tiles, buf, sem, p, j, count):
    def go(c, _):
        pltpu.make_async_copy(
            tiles.at[p, pl.ds(c * CH, CH)], buf.at[j, pl.ds(c * CH, CH)], sem.at[j, c]
        ).start()
        return 0

    lax.fori_loop(0, (count + CH - 1) // CH, go, 0)


def walk(tiles, buf, sem, p, j, count, group):
    def chunk(c, _):
        pltpu.make_async_copy(
            tiles.at[p, pl.ds(c * CH, CH)], buf.at[j, pl.ds(c * CH, CH)], sem.at[j, c]
        ).wait()
        left = jnp.minimum(count - c * CH, CH)
        lax.fori_loop(0, (left + U - 1) // U, lambda g, _: (group(c * CH + g * U), 0)[1], 0)
        return 0

    lax.fori_loop(0, (count + CH - 1) // CH, chunk, 0)


def degree_kernel(dests, counts, tiles, deg_out, buf, acc, sem):
    acc[...] = jnp.zeros_like(acc)
    ones = jnp.ones((8, T), bf16)
    for p in range(16):
        start_copies(tiles, buf, sem, p, p, counts[p])
    for p in range(16):
        count = counts[p]

        def group(first):
            sums, places = [], []
            for u in range(U):
                k = first + u
                places.append(jnp.where(k < count, dests[p * SLOTS + k], NDST))
                sums.append(
                    lax.dot_general(
                        ones, buf[p, k], (((1,), (1,)), ((), ())), preferred_element_type=f32
                    )
                )
            for u in range(U):
                acc[places[u]] += sums[u]

        walk(tiles, buf, sem, p, p, count, group)
    for d in range(NDST):
        deg_out[d : d + 1, :] = acc[d, 0:1, :]


def degrees(dests, counts, tiles):
    return pl.pallas_call(
        degree_kernel,
        name="degrees",
        out_shape=jax.ShapeDtypeStruct((NDST, T), f32),
        in_specs=[SMEM, SMEM, ANY],
        out_specs=VMEM,
        scratch_shapes=[
            pltpu.VMEM((16, SLOTS, T, T), bf16),
            pltpu.VMEM((NDST + 1, 8, T), f32),
            pltpu.SemaphoreType.DMA((16, SLOTS // CH)),
        ],
        compiler_params=params(),
        cost_estimate=pl.CostEstimate(flops=10**9, bytes_accessed=12 * 10**6, transcendentals=0),
    )(dests, counts, tiles)


def forward_kernel(places, first, last, *refs):
    n = len(places)
    dests, srcs, counts, tiles, deg, *refs = refs
    feats, refs = refs[:n], refs[n:]
    if not first:
        (acc_in, out, buf, acc, sem) = refs
    else:
        (out, buf, acc, sem) = refs
    parts = [blk_at(*w) for w in places]
    for j, p in enumerate(parts):
        start_copies(tiles, buf, sem, p, j, counts[p])
    if first:
        acc[...] = jnp.zeros_like(acc)
    else:
        acc[0:NDST] = acc_in[...]
    for j, p in enumerate(parts):
        count = counts[p]
        feat, row0 = feats[j]

        def group(k0):
            sums, where = [], []
            for u in range(U):
                k = k0 + u
                where.append(jnp.where(k < count, dests[p * SLOTS + k], NDST))
                row = pl.multiple_of(row0 + srcs[p * SLOTS + k] * T, T)
                sums.append(
                    jnp.dot(buf[j, k], feat[pl.ds(row, T), :], preferred_element_type=f32)
                )
            for u in range(U):
                acc[where[u]] += sums[u]

        walk(tiles, buf, sem, p, j, count, group)
    if not last:
        out[...] = acc[0:NDST]
    else:
        for m in range(REP):
            out[m, 0 : NSRC * T, :] = acc[m * NSRC : (m + 1) * NSRC].reshape(NSRC * T, T).astype(bf16)
            high, low = high_low(deg[m * NSRC : (m + 1) * NSRC, :])
            out[m, NSRC * T :, :] = jnp.concatenate(
                [high, low, jnp.zeros((DEG - 2 * NSRC, T), bf16)], axis=0
            )


def forward(places, blocks, dests, srcs, counts, tiles, deg, acc, last):
    n = len(places)
    first = acc is None
    rows = NSRC * T

    def kernel(*refs):
        head, refs = refs[:5], refs[5:]
        held, refs = refs[: len(blocks)], refs[len(blocks) :]
        feats = [
            (ref, i * rows) for ref, b in zip(held, blocks) for i in range(b.shape[0] // rows)
        ]
        forward_kernel(places, first, last, *head, *feats, *refs)

    if last:
        shape = jax.ShapeDtypeStruct((REP, rows + DEG, T), bf16)
    else:
        shape = jax.ShapeDtypeStruct((NDST, T, T), f32)
    extra = () if first else (acc,)
    return pl.pallas_call(
        kernel,
        name="forward_last" if last else "forward_first",
        out_shape=shape,
        in_specs=[SMEM, SMEM, SMEM, ANY, VMEM] + [VMEM] * (len(blocks) + len(extra)),
        out_specs=VMEM,
        scratch_shapes=[
            pltpu.VMEM((n, SLOTS, T, T), bf16),
            pltpu.VMEM((NDST + 1, T, T), f32),
            pltpu.SemaphoreType.DMA((n, SLOTS // CH)),
        ],
        compiler_params=params(),
        cost_estimate=pl.CostEstimate(
            flops=n * 17 * 2 * T**3, bytes_accessed=n * 17 * T * T * 2, transcendentals=0
        ),
    )(dests, srcs, counts, tiles, deg, *blocks, *extra)


def dense_kernel(recv, features, cotangent, w_self, w_neigh, bias, act, payload, self_t):
    rows = NSRC * T
    total = recv[0, 0:rows, :].astype(f32)
    deg = jnp.zeros((NSRC, T), f32)
    for m in range(REP):
        if m:
            total += recv[m, 0:rows, :].astype(f32)
        extra = recv[m, rows:, :].astype(f32)
        deg += extra[0:NSRC] + extra[NSRC : 2 * NSRC]
    scale = lax.rsqrt(1.0 + deg)
    eye = lax.broadcasted_iota(jnp.int32, (T, T), 0) == lax.broadcasted_iota(jnp.int32, (T, T), 1)
    columns = [
        jnp.sum(jnp.where(eye, scale[i : i + 1, :], 0.0), axis=1, keepdims=True) for i in range(NSRC)
    ]
    mean = (total * jnp.concatenate(columns, axis=0)).astype(bf16)
    feat = features[...]
    pre = (
        jnp.dot(feat, w_self[...], preferred_element_type=f32)
        + jnp.dot(mean, w_neigh[...], preferred_element_type=f32)
        + bias[...]
    )
    sigma = jax.nn.sigmoid(pre)
    act[...] = (pre * sigma).astype(bf16)
    grad = (cotangent[...].astype(f32) * sigma * (1.0 + pre * (1.0 - sigma))).astype(bf16)
    down = (((0,), (0,)), ((), ()))
    across = (((1,), (1,)), ((), ()))
    g_self = lax.dot_general(feat, grad, down, preferred_element_type=f32)
    g_neigh = lax.dot_general(mean, grad, down, preferred_element_type=f32)
    g_bias = jnp.sum(grad.astype(f32), axis=0, keepdims=True)
    sum_t = lax.dot_general(w_neigh[...], grad, across, preferred_element_type=f32)
    own_t = lax.dot_general(w_self[...], grad, across, preferred_element_type=f32)
    spread = []
    for i in range(NSRC):
        part = slice(i * T, (i + 1) * T)
        spread.append((sum_t[:, part] * scale[i : i + 1, :]).astype(bf16))
        self_t[i] = own_t[:, part]
    bias_rows = jnp.broadcast_to(g_bias, (8, T))
    for m in range(REP):
        for i in range(NSRC):
            payload[m, i * T : (i + 1) * T, :] = spread[i]
        piece = slice(m * 16, (m + 1) * 16)
        segment = jnp.concatenate([g_self[piece], g_neigh[piece], bias_rows], axis=0)
        payload[m, rows:, :] = jnp.concatenate(high_low(segment), axis=0)


def dense(recv, features, cotangent, w_self, w_neigh, bias):
    rows = NSRC * T
    return pl.pallas_call(
        dense_kernel,
        name="dense",
        out_shape=(
            jax.ShapeDtypeStruct((rows, T), bf16),
            jax.ShapeDtypeStruct((REP, rows + WX, T), bf16),
            jax.ShapeDtypeStruct((NSRC, T, T), f32),
        ),
        in_specs=[VMEM] * 6,
        out_specs=(VMEM, VMEM, VMEM),
        compiler_params=params(),
    )(recv, features, cotangent, w_self, w_neigh, bias.reshape(1, T))


def segment_of(rows):
    wide = rows.astype(f32)
    return wide[0:WROWS] + wide[WROWS:]


def backward_kernel(dz, first, dests, srcs, counts, tiles, recv, send, keep, buf, acc, sem):
    rows = NSRC * T
    places = [(0, dz, 1), (1, dz, 1), (0, dz, 0), (1, dz, 0)]
    parts = [blk_at(*w) for w in places]
    for j, p in enumerate(parts):
        start_copies(tiles, buf, sem, p, j, counts[p])
    acc[...] = jnp.zeros_like(acc)
    if first:
        total = segment_of(recv[0, rows:, :])
        for m in range(1, REP):
            total += segment_of(recv[m, rows:, :])
        send[2 * rows :, :] = jnp.concatenate(high_low(total), axis=0)
    for j, p in enumerate(parts):
        count = counts[p]

        def group(k0):
            sums, where = [], []
            for u in range(U):
                k = k0 + u
                where.append(jnp.where(k < count, srcs[p * SLOTS + k], NSRC))
                d = dests[p * SLOTS + k]
                row = pl.multiple_of(d % NSRC * T, T)
                sums.append(
                    jnp.dot(recv[d // NSRC, pl.ds(row, T), :], buf[j, k], preferred_element_type=f32)
                )
            for u in range(U):
                acc[j, where[u]] += sums[u]

        walk(tiles, buf, sem, p, j, count, group)
        whole = acc[j, 0:NSRC].reshape(rows, T)
        if j < 2:
            send[j * rows : (j + 1) * rows, :] = whole.astype(bf16)
        else:
            keep[(j - 2) * rows : (j - 1) * rows, :] = whole


def backward(dz, first, dests, srcs, counts, tiles, recv):
    rows = NSRC * T
    return pl.pallas_call(
        functools.partial(backward_kernel, dz, first),
        name=f"backward_z{dz}",
        out_shape=(
            jax.ShapeDtypeStruct((2 * rows + (WX if first else 0), T), bf16),
            jax.ShapeDtypeStruct((2 * rows, T), f32),
        ),
        in_specs=[SMEM, SMEM, SMEM, ANY, VMEM],
        out_specs=(VMEM, VMEM),
        scratch_shapes=[
            pltpu.VMEM((4, SLOTS, T, T), bf16),
            pltpu.VMEM((4, NSRC + 1, T, T), f32),
            pltpu.SemaphoreType.DMA((4, SLOTS // CH)),
        ],
        compiler_params=params(),
        cost_estimate=pl.CostEstimate(
            flops=4 * 17 * 2 * T**3, bytes_accessed=4 * 17 * T * T * 2, transcendentals=0
        ),
    )(dests, srcs, counts, tiles, recv)


def join_kernel(keep, got, seg, mine, out):
    rows = 2 * NSRC * T
    out[0:rows, :] = (keep[...] + got[0:rows, :].astype(f32)).astype(bf16)
    if mine is None:
        out[rows:, :] = seg[...]
    else:
        total = segment_of(mine[rows:, :]) + segment_of(got[rows:, :])
        out[rows:, :] = jnp.concatenate(high_low(total), axis=0)


def join(keep, got, seg=None, mine=None):
    rows = 2 * NSRC * T
    if mine is not None:
        body = lambda k, g, m, o: join_kernel(k, g, None, m, o)
        operands = (keep, got, mine)
    else:
        body = lambda k, g, s, o: join_kernel(k, g, s, None, o)
        operands = (keep, got, seg)
    return pl.pallas_call(
        body,
        name="join",
        out_shape=jax.ShapeDtypeStruct((rows + WX, T), bf16),
        in_specs=[VMEM] * 3,
        out_specs=VMEM,
        compiler_params=params(16),
    )(*operands)


def sum_kernel(keep, got, za, zb, zc, seg, near, far):
    rows = NSRC * T

    def total(lo, hi):
        v = keep[lo:hi, :] + got[lo:hi, :].astype(f32)
        for ref in (za, zb, zc):
            v += ref[lo:hi, :].astype(f32)
        return v

    near[0:rows, :] = total(0, rows)
    far[0:rows, :] = total(rows, 2 * rows).astype(bf16)
    s = segment_of(seg[...])
    for ref in (za, zb, zc):
        s += segment_of(ref[2 * rows :, :])
    near[rows:, :] = s
    far[rows:, :] = jnp.concatenate(high_low(s), axis=0)


def sum_up(keep, got, za, zb, zc, seg):
    rows = NSRC * T
    return pl.pallas_call(
        sum_kernel,
        name="sum_up",
        out_shape=(
            jax.ShapeDtypeStruct((rows + WROWS, T), f32),
            jax.ShapeDtypeStruct((rows + WX, T), bf16),
        ),
        in_specs=[VMEM] * 6,
        out_specs=(VMEM, VMEM),
        compiler_params=params(16),
    )(keep, got, za, zb, zc, seg)


def final_kernel(near, far, self_t, out, seg):
    rows = NSRC * T
    for i in range(NSRC):
        part = slice(i * T, (i + 1) * T)
        block = near[part, :] + far[part, :].astype(f32) + self_t[i]
        out[part, :] = block.T
    seg[...] = near[rows:, :] + segment_of(far[rows:, :])


def final(near, far, self_t):
    rows = NSRC * T
    return pl.pallas_call(
        final_kernel,
        name="final",
        out_shape=(
            jax.ShapeDtypeStruct((rows, T), f32),
            jax.ShapeDtypeStruct((WROWS, T), f32),
        ),
        in_specs=[VMEM] * 3,
        out_specs=(VMEM, VMEM),
        compiler_params=params(16),
    )(near, far, self_t)


def shards(
    features, cotangent, w_self, w_neigh, out_bias, tile_values, dest_tile, src_tile, tile_count
):
    tiles = tile_values[0, 0]
    dests, srcs, counts = dest_tile.reshape(-1), src_tile.reshape(-1), tile_count.reshape(-1)
    rows = NSRC * T

    opposite = moved(features, 1, 0, 0)
    pair = jnp.concatenate([features, opposite], axis=0)
    za, zb, zc = moved(pair, 0, 2, 0), moved(pair, 0, 1, 0), moved(pair, 0, 3, 0)
    deg = degrees(dests, counts, tiles)
    held = (pair, za, zb, zc)
    others = tuple(moved(h, 0, 0, 1) for h in held)
    near_places = [(x, z, 0) for z in (0, -2, -1, -3) for x in (0, 1)]
    far_places = [(x, z, 1) for z in (0, -2, -1, -3) for x in (0, 1)]
    acc = forward(near_places, held, dests, srcs, counts, tiles, deg, None, False)
    sums = forward(far_places, others, dests, srcs, counts, tiles, deg, acc, True)
    recv = lax.all_to_all(sums, "rep", 0, 0)

    act, payload, self_t = dense(recv, features, cotangent, w_self, w_neigh, out_bias)
    spread = lax.all_to_all(payload, "rep", 0, 0)

    seg = None
    joined = []
    for dz in (2, 1, 3, 0):
        send, keep = backward(dz, dz == 2, dests, srcs, counts, tiles, spread)
        got = moved(send, 0, 0, 1)
        if dz == 0:
            break
        if seg is None:
            out = join(keep, got, mine=send)
            seg = out[2 * rows :]
        else:
            out = join(keep, got, seg=seg)
        joined.append(moved(out, 0, dz, 0))
    near, far = sum_up(keep, got, *joined, seg)
    grad_features, segment = final(near, moved(far, 1, 0, 0), self_t)
    weights = lax.all_to_all(jnp.broadcast_to(segment[None, 0:32], (REP, 32, T)), "rep", 0, 0)
    grad_w_self = weights[:, 0:16].reshape(T, T)
    grad_w_neigh = weights[:, 16:32].reshape(T, T)
    return (act, grad_features, grad_w_self, grad_w_neigh, segment[32])


def solution(mesh):
    placed = (
        P(("blk", "rep"), None),
        P(("blk", "rep"), None),
        P(),
        P(),
        P(),
        P("blk", "rep", None, None, None, None),
        P("blk", "rep", None, None),
        P("blk", "rep", None, None),
        P("blk", "rep", None),
    )
    return jax.shard_map(
        shards,
        mesh=mesh,
        in_specs=placed,
        out_specs=(P(("blk", "rep"), None), P(("blk", "rep"), None), P(), P(), P()),
        check_vma=False,
    )
```

```python
import functools

import jax
import jax.numpy as jnp
from jax import lax
from jax.experimental import pallas as pl
from jax.experimental.pallas import tpu as pltpu
from jax.sharding import PartitionSpec as P

f32, bf16 = jnp.float32, jnp.bfloat16
T = 128
SLOTS = 32
NSRC = 4
NDST = 32
REP = 8
CH = 8
BIG, SMALL = 32, 8
DEG = 16
WROWS = 72
WX = 2 * WROWS
SMEM = pl.BlockSpec(memory_space=pltpu.SMEM)
VMEM = pl.BlockSpec(memory_space=pltpu.VMEM)
ANY = pl.BlockSpec(memory_space=pl.ANY)
HBM = pl.BlockSpec(memory_space=pltpu.HBM)


def params(mib=24):
    return pltpu.CompilerParams(vmem_limit_bytes=mib * 1024 * 1024)


def blk_at(dx, dz, dc):
    here = lax.axis_index("blk")
    x, z, c = here // 8, (here // 2) % 4, here % 2
    return (x + dx) % 2 * 8 + (z + dz) % 4 * 2 + (c + dc) % 2


def moved(value, dx, dz, dc):
    pairs = []
    for i in range(16):
        x, z, c = i // 8, (i // 2) % 4, i % 2
        pairs.append((i, (x + dx) % 2 * 8 + (z + dz) % 4 * 2 + (c + dc) % 2))
    return lax.ppermute(value, "blk", pairs)


def moved_y(value, dy):
    return lax.ppermute(value, "rep", [(i, (i // 2 + dy) % 4 * 2 + i % 2) for i in range(REP)])


def high_low(v):
    high = v.astype(bf16)
    return high, (v - high.astype(f32)).astype(bf16)


def walk(entries, base, count, group):
    def step(first, size):
        group([entries[first + u] for u in range(size)])
        return 0

    whole = count // BIG
    lax.fori_loop(0, whole, lambda g, _: step(base + g * BIG, BIG), 0)
    rest = (count - whole * BIG + SMALL - 1) // SMALL
    lax.fori_loop(0, rest, lambda g, _: step(base + whole * BIG + g * SMALL, SMALL), 0)


STEPS = (2, 1, 3, 0)
CAP = 8 * SLOTS + SMALL


def group_parts(dx):
    return [blk_at(dx, dz, dc) for dc in (0, 1) for dz in STEPS]


def slot_of(entry):
    return entry & 511


def column_of(entry):
    return (entry >> 5) & 127


def dest_of(entry):
    return entry >> 12


def make_plan(dests, srcs, counts, entries, totals):
    none = lax.axis_index("blk") * SLOTS + NSRC * 512 + NDST * 4096
    for dx in range(2):
        end = dx * CAP
        for p in group_parts(dx):

            def put(g, _, p=p, end=end):
                for u in range(8):
                    k = g * 8 + u
                    entries[end + k] = p * SLOTS + k + (srcs[0, 0, p, k] << 9) + (dests[0, 0, p, k] << 12)
                return 0

            count = counts[0, 0, p]
            lax.fori_loop(0, (count + 7) // 8, put, 0)
            end = end + count
        for u in range(SMALL):
            entries[end + u] = none
        totals[dx] = end - dx * CAP


def load_kernel(
    dests_in, srcs_in, counts_in, tiles, after, held, deg_out, entries, totals, acc, sem, dests, srcs, counts, small_sem
):
    pairs = ((counts_in, counts), (dests_in, dests), (srcs_in, srcs))
    small = [pltpu.make_async_copy(a, b, small_sem.at[i]) for i, (a, b) in enumerate(pairs)]
    for copy in small:
        copy.start()
    small[0].wait()

    def each_copy(p, act):
        def go(c, _):
            part = pl.ds(pl.multiple_of(p * SLOTS + c * CH, CH), CH)
            act(pltpu.make_async_copy(tiles.at[p, pl.ds(c * CH, CH)], held.at[part], sem.at[p, c]))
            return 0

        lax.fori_loop(0, (counts[0, 0, p] + CH - 1) // CH, go, 0)

    for p in range(16):
        each_copy(p, lambda copy: copy.start())
    small[1].wait()
    small[2].wait()
    make_plan(dests, srcs, counts, entries, totals)
    acc[...] = jnp.zeros_like(acc)

    def add(p, _):
        each_copy(p, lambda copy: copy.wait())
        count = counts[0, 0, p]

        def step(g, _):
            for u in range(SMALL):
                k = g * SMALL + u
                d = jnp.where(k < count, dests[0, 0, p, k], NDST)
                acc[d] += held[p * SLOTS + k].astype(f32)
            return 0

        lax.fori_loop(0, (count + SMALL - 1) // SMALL, step, 0)
        return 0

    lax.fori_loop(0, 16, add, 0)
    eye = lax.broadcasted_iota(jnp.int32, (T, T), 0) == lax.broadcasted_iota(jnp.int32, (T, T), 1)
    for d in range(NDST):
        column = jnp.sum(acc[d], axis=1, keepdims=True)
        deg_out[d : d + 1, :] = jnp.sum(jnp.where(eye, column, 0.0), axis=0, keepdims=True)


def load(dest_tile, src_tile, tile_count, tiles, after):
    return pl.pallas_call(
        load_kernel,
        name="load",
        out_shape=(
            jax.ShapeDtypeStruct((16 * SLOTS, T, T), bf16),
            jax.ShapeDtypeStruct((NDST, T), f32),
            jax.ShapeDtypeStruct((2 * CAP,), jnp.int32),
            jax.ShapeDtypeStruct((2,), jnp.int32),
        ),
        in_specs=[HBM] * 4 + [ANY],
        out_specs=(VMEM, VMEM, SMEM, SMEM),
        scratch_shapes=[
            pltpu.VMEM((NDST + 1, T, T), f32),
            pltpu.SemaphoreType.DMA((16, SLOTS // CH)),
            pltpu.SMEM(dest_tile.shape, jnp.int32),
            pltpu.SMEM(src_tile.shape, jnp.int32),
            pltpu.SMEM(tile_count.shape, jnp.int32),
            pltpu.SemaphoreType.DMA((3,)),
        ],
        compiler_params=params(),
        cost_estimate=pl.CostEstimate(flops=10**10, bytes_accessed=12 * 10**6, transcendentals=0),
    )(dest_tile, src_tile, tile_count, tiles, after)


def small_call(body, name, shapes, *operands, after=()):
    n = len(operands)
    return pl.pallas_call(
        lambda *refs: body(*refs[:n], *refs[n + len(after) :]),
        name=name,
        out_shape=shapes,
        in_specs=[VMEM] * n + [ANY] * len(after),
        out_specs=VMEM if isinstance(shapes, jax.ShapeDtypeStruct) else (VMEM,) * len(shapes),
        compiler_params=params(8),
    )(*operands, *after)


def glue(parts, after=()):
    def body(*refs):
        *parts, out = refs
        row = 0
        for part in parts:
            out[row : row + part.shape[0], :] = part[...]
            row += part.shape[0]

    shape = jax.ShapeDtypeStruct((sum(p.shape[0] for p in parts), T), bf16)
    return small_call(body, "glue", shape, *parts, after=after)


def forward_kernel(dx, after, entries, totals, tiles, mine, other, *refs):
    rows = NSRC * T
    if dx:
        acc_in, deg, out, acc, feat = refs
        acc[0:NDST] = acc_in[0:NDST]
    else:
        acc, feat = refs
        acc[...] = jnp.zeros_like(acc)
    for j, p in enumerate(group_parts(dx)):
        ref, first = (mine, other)[j // 4], j % 4 * rows
        for t in range(NSRC):
            feat[t * 16 + p] = ref[first + t * T : first + (t + 1) * T, :]

    def group(words):
        sums = [
            jnp.dot(tiles[slot_of(w)], feat[column_of(w)], preferred_element_type=f32) for w in words
        ]
        for w, s in zip(words, sums):
            acc[dest_of(w)] += s

    walk(entries, dx * CAP, totals[dx], group)
    if dx:
        for m in range(REP):
            out[m, 0:rows, :] = acc[m * NSRC : (m + 1) * NSRC].reshape(rows, T).astype(bf16)
            high, low = high_low(deg[m * NSRC : (m + 1) * NSRC, :])
            out[m, rows:, :] = jnp.concatenate(
                [high, low, jnp.zeros((DEG - 2 * NSRC, T), bf16)], axis=0
            )


def forward(dx, after, entries, totals, tiles, mine, other, *extra):
    rows = NSRC * T
    sums = (NDST + 1, T, T)
    if dx:
        shape = jax.ShapeDtypeStruct((REP, rows + DEG, T), bf16)
    else:
        shape = jax.ShapeDtypeStruct(sums, f32)
    return pl.pallas_call(
        functools.partial(forward_kernel, dx),
        name=f"forward_{dx}",
        out_shape=shape,
        in_specs=[ANY, SMEM, SMEM] + [VMEM] * (3 + len(extra)),
        out_specs=VMEM,
        scratch_shapes=([pltpu.VMEM(sums, f32)] if dx else []) + [pltpu.VMEM((80, T, T), bf16)],
        compiler_params=params(),
        cost_estimate=pl.CostEstimate(
            flops=4 * 10**9, bytes_accessed=8 * 17 * T * T * 2, transcendentals=0
        ),
    )(after, entries, totals, tiles, mine, other, *extra)


def dense_kernel(recv, features, cotangent, w_self, w_neigh, bias, act, payload, self_t):
    rows = NSRC * T
    total = recv[0, 0:rows, :].astype(f32)
    deg = jnp.zeros((NSRC, T), f32)
    for m in range(REP):
        if m:
            total += recv[m, 0:rows, :].astype(f32)
        extra = recv[m, rows:, :].astype(f32)
        deg += extra[0:NSRC] + extra[NSRC : 2 * NSRC]
    scale = lax.rsqrt(1.0 + deg)
    eye = lax.broadcasted_iota(jnp.int32, (T, T), 0) == lax.broadcasted_iota(jnp.int32, (T, T), 1)
    columns = [
        jnp.sum(jnp.where(eye, scale[i : i + 1, :], 0.0), axis=1, keepdims=True) for i in range(NSRC)
    ]
    mean = (total * jnp.concatenate(columns, axis=0)).astype(bf16)
    feat = features[...]
    pre = (
        jnp.dot(feat, w_self[...], preferred_element_type=f32)
        + jnp.dot(mean, w_neigh[...], preferred_element_type=f32)
        + bias[...]
    )
    sigma = jax.nn.sigmoid(pre)
    act[...] = (pre * sigma).astype(bf16)
    grad = (cotangent[...].astype(f32) * sigma * (1.0 + pre * (1.0 - sigma))).astype(bf16)
    down = (((0,), (0,)), ((), ()))
    across = (((1,), (1,)), ((), ()))
    g_self = lax.dot_general(feat, grad, down, preferred_element_type=f32)
    g_neigh = lax.dot_general(mean, grad, down, preferred_element_type=f32)
    g_bias = jnp.sum(grad.astype(f32), axis=0, keepdims=True)
    sum_t = lax.dot_general(w_neigh[...], grad, across, preferred_element_type=f32)
    own_t = lax.dot_general(w_self[...], grad, across, preferred_element_type=f32)
    spread = []
    for i in range(NSRC):
        part = slice(i * T, (i + 1) * T)
        spread.append((sum_t[:, part] * scale[i : i + 1, :]).astype(bf16))
        self_t[i] = own_t[:, part]
    bias_rows = jnp.broadcast_to(g_bias, (8, T))
    for m in range(REP):
        for i in range(NSRC):
            payload[m, i * T : (i + 1) * T, :] = spread[i]
        piece = slice(m // 2 * 32, (m // 2 + 1) * 32)
        segment = jnp.concatenate([g_self[piece], g_neigh[piece], bias_rows], axis=0)
        payload[m, rows:, :] = jnp.concatenate(high_low(segment), axis=0)


def dense(recv, features, cotangent, w_self, w_neigh, bias):
    rows = NSRC * T
    return pl.pallas_call(
        dense_kernel,
        name="dense",
        out_shape=(
            jax.ShapeDtypeStruct((rows, T), bf16),
            jax.ShapeDtypeStruct((REP, rows + WX, T), bf16),
            jax.ShapeDtypeStruct((NSRC, T, T), f32),
        ),
        in_specs=[VMEM] * 6,
        out_specs=(VMEM, VMEM, VMEM),
        compiler_params=params(),
    )(recv, features, cotangent, w_self, w_neigh, bias.reshape(1, T))


def segment_of(rows):
    wide = rows.astype(f32)
    return wide[0:WROWS] + wide[WROWS:]


def backward_kernel(entries, totals, tiles, recv, send, keep, acc):
    rows = NSRC * T
    parts = group_parts(1) + group_parts(0)
    acc[...] = jnp.zeros_like(acc)

    def group(words):
        sums = []
        for w in words:
            d = dest_of(w) & (NDST - 1)
            row = pl.multiple_of((d & (NSRC - 1)) << 7, T)
            sums.append(
                jnp.dot(recv[d >> 2, pl.ds(row, T), :], tiles[slot_of(w)], preferred_element_type=f32)
            )
        for w, s in zip(words, sums):
            acc[column_of(w)] += s

    for dx in (1, 0):
        walk(entries, dx * CAP, totals[dx], group)
    for j, p in enumerate(parts):
        first = (j // 8 * 4 + j % 4) * rows
        for t in range(NSRC):
            to = slice(first + t * T, first + (t + 1) * T)
            if j % 8 < 4:
                keep[to, :] = acc[t * 16 + p]
            else:
                send[to, :] = acc[t * 16 + p].astype(bf16)


def backward(entries, totals, tiles, recv):
    rows = NSRC * T
    return pl.pallas_call(
        backward_kernel,
        name="backward",
        out_shape=(
            jax.ShapeDtypeStruct((8 * rows, T), bf16),
            jax.ShapeDtypeStruct((8 * rows, T), f32),
        ),
        in_specs=[SMEM, SMEM, VMEM, VMEM],
        out_specs=(VMEM, VMEM),
        scratch_shapes=[pltpu.VMEM((80, T, T), f32)],
        compiler_params=params(),
        cost_estimate=pl.CostEstimate(
            flops=8 * 10**9, bytes_accessed=16 * 17 * T * T * 2, transcendentals=0
        ),
    )(entries, totals, tiles, recv)


def append(send, seg, seg_got):
    n = send.shape[0]

    def body(send, seg, got, out):
        out[0:n, :] = send[...]
        out[n:, :] = jnp.concatenate(high_low(segment_of(seg[...]) + segment_of(got[...])), axis=0)

    return small_call(body, "append", jax.ShapeDtypeStruct((n + WX, T), bf16), send, seg, seg_got)


def core_sums(keep, got, sent):
    rows = NSRC * T
    high = rows + WX

    def body(keep, got, sent, *out):
        for i, ref in enumerate(out):
            part = slice(i * rows, (i + 1) * rows)
            value = keep[part, :] + got[part, :].astype(f32)
            ref[0:rows, :] = value.astype(ref.dtype)
        total = segment_of(got[8 * rows :, :]) + segment_of(sent[8 * rows :, :])
        total = jnp.concatenate(high_low(total), axis=0)
        for ref in out[0:3]:
            ref[rows:, :] = total

    shapes = [jax.ShapeDtypeStruct((high, T), bf16)] * 3 + [jax.ShapeDtypeStruct((rows, T), f32)]
    shapes += [jax.ShapeDtypeStruct((rows, T), bf16)] * 3 + [jax.ShapeDtypeStruct((rows, T), f32)]
    return small_call(body, "core_sums", tuple(shapes), keep, got, sent)


def member_segments(spread):
    rows = NSRC * T

    def body(spread, out):
        total = segment_of(spread[0, rows:, :])
        for m in range(1, REP):
            total += segment_of(spread[m, rows:, :])
        out[...] = jnp.concatenate(high_low(total), axis=0)

    return small_call(body, "member_segments", jax.ShapeDtypeStruct((WX, T), bf16), spread)


def z_sum(near, *parts):
    rows = NSRC * T

    def body(near, a, b, c, far):
        block = near[...]
        for ref in (a, b, c):
            block += ref[0:rows, :].astype(f32)
        far[...] = block.astype(bf16)

    return small_call(body, "z_sum", jax.ShapeDtypeStruct((rows, T), bf16), near, *parts)


def z_segments(own, *parts, after):
    rows = NSRC * T

    def body(own, a, b, c, pieces, bias):
        total = segment_of(own[rows:, :])
        for ref in (a, b, c):
            total += segment_of(ref[rows:, :])
        pieces[...] = total[0:64]
        bias[...] = total[64:65]

    shapes = (jax.ShapeDtypeStruct((64, T), f32), jax.ShapeDtypeStruct((1, T), f32))
    return small_call(body, "z_segments", shapes, own, *parts, after=after)


def final(pieces, near, self_t, *others):
    rows = NSRC * T

    def body(p0, p1, p2, p3, near, self_t, *refs):
        *others, out, w_self, w_neigh = refs
        for i in range(NSRC):
            part = slice(i * T, (i + 1) * T)
            block = near[part, :] + self_t[i]
            for other in others:
                block += other[part, :].astype(f32)
            out[part, :] = block.T
        y = lax.axis_index("rep") // 2
        for back, piece in enumerate((p0, p1, p2, p3)):
            to = pl.ds(pl.multiple_of((y - back) % 4 * 32, 32), 32)
            w_self[to, :] = piece[0:32]
            w_neigh[to, :] = piece[32:64]

    shapes = (jax.ShapeDtypeStruct((rows, T), f32),) + (jax.ShapeDtypeStruct((T, T), f32),) * 2
    return small_call(body, "final", shapes, *pieces, near, self_t, *others)


def shards(
    features, cotangent, w_self, w_neigh, out_bias, tile_values, dest_tile, src_tile, tile_count
):
    rows = NSRC * T

    opposite = glue([moved(features, 1, 0, 0)])
    near = glue([moved(features, 0, -dz, 0) if dz else features for dz in STEPS])
    far = [moved(opposite, 0, -dz, 0) if dz else opposite for dz in STEPS]
    tiles, deg, entries, totals = load(dest_tile, src_tile, tile_count, tile_values[0, 0], near)
    far = glue(far, (deg,))
    acc = forward(0, far, entries, totals, tiles, near, moved(near, 0, 0, 1))
    sums = forward(1, acc, entries, totals, tiles, far, moved(far, 0, 0, 1), acc, deg)
    recv = lax.all_to_all(sums, "rep", 0, 0)

    act, payload, self_t = dense(recv, features, cotangent, w_self, w_neigh, out_bias)
    spread = lax.all_to_all(payload, "rep", 0, 0)

    seg = member_segments(spread)
    seg_got = moved(seg, 1, 0, 0)
    send, keep = backward(entries, totals, tiles, spread)
    send = append(send, seg, seg_got)
    out = core_sums(keep, moved(send, 0, 0, 1), send)
    far_out, far_block, near_out, near_block = out[0:3], out[3], out[4:7], out[7]
    far_parts = [moved(v, 0, dz, 0) for v, dz in zip(far_out, STEPS)]
    near_parts = [moved(v, 0, dz, 0) for v, dz in zip(near_out, STEPS)]
    far = z_sum(far_block, *far_parts)
    pieces, bias = z_segments(far_out[0], *far_parts, after=(far,))
    pieces = [pieces] + [moved_y(pieces, dy) for dy in (1, 2, 3)]
    grad_features, grad_w_self, grad_w_neigh = final(
        pieces, near_block, self_t, moved(far, 1, 0, 0), *near_parts
    )
    return (act, grad_features, grad_w_self, grad_w_neigh, bias.reshape(T))


def solution(mesh):
    placed = (
        P(("blk", "rep"), None),
        P(("blk", "rep"), None),
        P(),
        P(),
        P(),
        P("blk", "rep", None, None, None, None),
        P("blk", "rep", None, None),
        P("blk", "rep", None, None),
        P("blk", "rep", None),
    )
    return jax.shard_map(
        shards,
        mesh=mesh,
        in_specs=placed,
        out_specs=(P(("blk", "rep"), None), P(("blk", "rep"), None), P(), P(), P()),
        check_vma=False,
    )
```

```python
import functools

import jax
import jax.numpy as jnp
from jax import lax
from jax.experimental import pallas as pl
from jax.experimental.pallas import tpu as pltpu
from jax.sharding import PartitionSpec as P

f32, bf16 = jnp.float32, jnp.bfloat16
T = 128
SLOTS = 32
NSRC = 4
NDST = 32
REP = 8
CH = 8
STEP_SIZES = (64, 32, 16, 8)
SMALL = STEP_SIZES[-1]
DEG = 16
WROWS = 72
WX = 2 * WROWS
WB = 80
SMEM = pl.BlockSpec(memory_space=pltpu.SMEM)
VMEM = pl.BlockSpec(memory_space=pltpu.VMEM)
ANY = pl.BlockSpec(memory_space=pl.ANY)
HBM = pl.BlockSpec(memory_space=pltpu.HBM)


def params(mib=24):
    return pltpu.CompilerParams(vmem_limit_bytes=mib * 1024 * 1024)


def blk_at(dx, dz, dc):
    here = lax.axis_index("blk")
    x, z, c = here // 8, (here // 2) % 4, here % 2
    return (x + dx) % 2 * 8 + (z + dz) % 4 * 2 + (c + dc) % 2


def moved(value, dx, dz, dc):
    pairs = []
    for i in range(16):
        x, z, c = i // 8, (i // 2) % 4, i % 2
        pairs.append((i, (x + dx) % 2 * 8 + (z + dz) % 4 * 2 + (c + dc) % 2))
    return lax.ppermute(value, "blk", pairs)


def moved_y(value, dy):
    return lax.ppermute(value, "rep", [(i, (i // 2 + dy) % 4 * 2 + i % 2) for i in range(REP)])


def high_low(v):
    high = v.astype(bf16)
    return high, (v - high.astype(f32)).astype(bf16)


def walk(entries, base, count, group):
    def step(first, size):
        group([entries[first + u] for u in range(size)])
        return 0

    end = base + count
    for size in STEP_SIZES:
        steps = (end - base + (size - 1 if size == SMALL else 0)) // size
        lax.fori_loop(0, steps, lambda g, _, base=base, size=size: step(base + g * size, size), 0)
        base = base + steps * size


STEPS = (2, 1, 3, 0)
CAP = 8 * SLOTS + SMALL


def group_parts(dc):
    return [blk_at(dx, dz, dc) for dx in (1, 0) for dz in STEPS]


def slot_of(entry):
    return entry & 511


def column_of(entry):
    return (entry >> 5) & 127


def dest_of(entry):
    return entry >> 12


def make_plan(dests, srcs, counts, entries, totals):
    none = lax.axis_index("blk") * SLOTS + NSRC * 512 + NDST * 4096
    for dc in range(2):
        end = dc * CAP
        for p in group_parts(dc):

            def put(g, _, p=p, end=end):
                for u in range(8):
                    k = g * 8 + u
                    entries[end + k] = p * SLOTS + k + (srcs[0, 0, p, k] << 9) + (dests[0, 0, p, k] << 12)
                return 0

            count = counts[0, 0, p]
            lax.fori_loop(0, (count + 7) // 8, put, 0)
            end = end + count
        for u in range(SMALL):
            entries[end + u] = none
        totals[dc] = end - dc * CAP


def load_kernel(
    dests_in, srcs_in, counts_in, tiles, after, held, deg_out, entries, totals, acc, sem, dests, srcs, counts, small_sem
):
    pairs = ((counts_in, counts), (dests_in, dests), (srcs_in, srcs))
    small = [pltpu.make_async_copy(a, b, small_sem.at[i]) for i, (a, b) in enumerate(pairs)]
    for copy in small:
        copy.start()
    small[0].wait()

    def each_copy(p, act):
        def go(c, _):
            part = pl.ds(pl.multiple_of(p * SLOTS + c * CH, CH), CH)
            act(pltpu.make_async_copy(tiles.at[p, pl.ds(c * CH, CH)], held.at[part], sem.at[p, c]))
            return 0

        lax.fori_loop(0, (counts[0, 0, p] + CH - 1) // CH, go, 0)

    for p in range(16):
        each_copy(p, lambda copy: copy.start())
    small[1].wait()
    small[2].wait()
    make_plan(dests, srcs, counts, entries, totals)
    acc[...] = jnp.zeros_like(acc)

    def add(p, _):
        each_copy(p, lambda copy: copy.wait())
        count = counts[0, 0, p]

        def step(g, _):
            for u in range(SMALL):
                k = g * SMALL + u
                d = jnp.where(k < count, dests[0, 0, p, k], NDST)
                acc[d] += held[p * SLOTS + k].astype(f32)
            return 0

        lax.fori_loop(0, (count + SMALL - 1) // SMALL, step, 0)
        return 0

    lax.fori_loop(0, 16, add, 0)
    eye = lax.broadcasted_iota(jnp.int32, (T, T), 0) == lax.broadcasted_iota(jnp.int32, (T, T), 1)
    for d in range(NDST):
        column = jnp.sum(acc[d], axis=1, keepdims=True)
        deg_out[d : d + 1, :] = jnp.sum(jnp.where(eye, column, 0.0), axis=0, keepdims=True)


def load(dest_tile, src_tile, tile_count, tiles, after):
    return pl.pallas_call(
        load_kernel,
        name="load",
        out_shape=(
            jax.ShapeDtypeStruct((16 * SLOTS, T, T), bf16),
            jax.ShapeDtypeStruct((NDST, T), f32),
            jax.ShapeDtypeStruct((2 * CAP,), jnp.int32),
            jax.ShapeDtypeStruct((2,), jnp.int32),
        ),
        in_specs=[HBM] * 4 + [ANY],
        out_specs=(VMEM, VMEM, SMEM, SMEM),
        scratch_shapes=[
            pltpu.VMEM((NDST + 1, T, T), f32),
            pltpu.SemaphoreType.DMA((16, SLOTS // CH)),
            pltpu.SMEM(dest_tile.shape, jnp.int32),
            pltpu.SMEM(src_tile.shape, jnp.int32),
            pltpu.SMEM(tile_count.shape, jnp.int32),
            pltpu.SemaphoreType.DMA((3,)),
        ],
        compiler_params=params(),
        cost_estimate=pl.CostEstimate(flops=10**10, bytes_accessed=12 * 10**6, transcendentals=0),
    )(dest_tile, src_tile, tile_count, tiles, after)


def small_call(body, name, shapes, *operands, after=()):
    n = len(operands)
    return pl.pallas_call(
        lambda *refs: body(*refs[:n], *refs[n + len(after) :]),
        name=name,
        out_shape=shapes,
        in_specs=[VMEM] * n + [ANY] * len(after),
        out_specs=VMEM if isinstance(shapes, jax.ShapeDtypeStruct) else (VMEM,) * len(shapes),
        compiler_params=params(8),
    )(*operands, *after)


def glue(parts, after=()):
    arrays = []
    for array, _, _ in parts:
        if not any(array is a for a in arrays):
            arrays.append(array)

    def body(*refs):
        *refs, out = refs
        row = 0
        for array, first, rows in parts:
            ref = refs[[array is a for a in arrays].index(True)]
            out[row : row + rows, :] = ref[first : first + rows, :]
            row += rows

    shape = jax.ShapeDtypeStruct((sum(rows for _, _, rows in parts), T), bf16)
    return small_call(body, "glue", shape, *arrays, after=after)


def forward_kernel(dc, entries, totals, tiles, blocks, *refs):
    rows = NSRC * T
    if dc:
        acc_in, deg, out, acc, feat = refs
        acc[0:NDST] = acc_in[0:NDST]
    else:
        acc, feat = refs
        acc[...] = jnp.zeros_like(acc)
    for j, p in enumerate(group_parts(dc)):
        for t in range(NSRC):
            feat[t * 16 + p] = blocks[j * rows + t * T : j * rows + (t + 1) * T, :]

    def group(words):
        sums = [
            jnp.dot(tiles[slot_of(w)], feat[column_of(w)], preferred_element_type=f32) for w in words
        ]
        for w, s in zip(words, sums):
            acc[dest_of(w)] += s

    walk(entries, dc * CAP, totals[dc], group)
    if dc:
        for m in range(REP):
            out[m, 0:rows, :] = acc[m * NSRC : (m + 1) * NSRC].reshape(rows, T).astype(bf16)
            high, low = high_low(deg[m * NSRC : (m + 1) * NSRC, :])
            out[m, rows:, :] = jnp.concatenate(
                [high, low, jnp.zeros((DEG - 2 * NSRC, T), bf16)], axis=0
            )


def forward(dc, entries, totals, tiles, blocks, *extra):
    rows = NSRC * T
    sums = (NDST + 1, T, T)
    if dc:
        shape = jax.ShapeDtypeStruct((REP, rows + DEG, T), bf16)
    else:
        shape = jax.ShapeDtypeStruct(sums, f32)
    return pl.pallas_call(
        functools.partial(forward_kernel, dc),
        name=f"forward_{dc}",
        out_shape=shape,
        in_specs=[SMEM, SMEM] + [VMEM] * (2 + len(extra)),
        out_specs=VMEM,
        scratch_shapes=([pltpu.VMEM(sums, f32)] if dc else []) + [pltpu.VMEM((80, T, T), bf16)],
        compiler_params=params(),
        cost_estimate=pl.CostEstimate(
            flops=4 * 10**9, bytes_accessed=8 * 17 * T * T * 2, transcendentals=0
        ),
    )(entries, totals, tiles, blocks, *extra)


def dense_kernel(recv, features, cotangent, w_self, w_neigh, bias, act, payload, self_t):
    rows = NSRC * T
    total = recv[0, 0:rows, :].astype(f32)
    deg = jnp.zeros((NSRC, T), f32)
    for m in range(REP):
        if m:
            total += recv[m, 0:rows, :].astype(f32)
        extra = recv[m, rows:, :].astype(f32)
        deg += extra[0:NSRC] + extra[NSRC : 2 * NSRC]
    scale = lax.rsqrt(1.0 + deg)
    eye = lax.broadcasted_iota(jnp.int32, (T, T), 0) == lax.broadcasted_iota(jnp.int32, (T, T), 1)
    columns = [
        jnp.sum(jnp.where(eye, scale[i : i + 1, :], 0.0), axis=1, keepdims=True) for i in range(NSRC)
    ]
    mean = (total * jnp.concatenate(columns, axis=0)).astype(bf16)
    feat = features[...]
    pre = (
        jnp.dot(feat, w_self[...], preferred_element_type=f32)
        + jnp.dot(mean, w_neigh[...], preferred_element_type=f32)
        + bias[...]
    )
    sigma = jax.nn.sigmoid(pre)
    act[...] = (pre * sigma).astype(bf16)
    grad = (cotangent[...].astype(f32) * sigma * (1.0 + pre * (1.0 - sigma))).astype(bf16)
    down = (((0,), (0,)), ((), ()))
    across = (((1,), (1,)), ((), ()))
    g_self = lax.dot_general(feat, grad, down, preferred_element_type=f32)
    g_neigh = lax.dot_general(mean, grad, down, preferred_element_type=f32)
    g_bias = jnp.sum(grad.astype(f32), axis=0, keepdims=True)
    sum_t = lax.dot_general(w_neigh[...], grad, across, preferred_element_type=f32)
    own_t = lax.dot_general(w_self[...], grad, across, preferred_element_type=f32)
    spread = []
    for i in range(NSRC):
        part = slice(i * T, (i + 1) * T)
        spread.append((sum_t[:, part] * scale[i : i + 1, :]).astype(bf16))
        self_t[i] = own_t[:, part]
    bias_rows = jnp.broadcast_to(g_bias, (8, T))
    for m in range(REP):
        for i in range(NSRC):
            payload[m, i * T : (i + 1) * T, :] = spread[i]
        piece = slice(m // 2 * 32, (m // 2 + 1) * 32)
        segment = [g_self[piece], g_neigh[piece], bias_rows, jnp.zeros((WB - WROWS, T), f32)]
        payload[m, rows:, :] = jnp.concatenate(segment, axis=0).astype(bf16)


def dense(recv, features, cotangent, w_self, w_neigh, bias):
    rows = NSRC * T
    return pl.pallas_call(
        dense_kernel,
        name="dense",
        out_shape=(
            jax.ShapeDtypeStruct((rows, T), bf16),
            jax.ShapeDtypeStruct((REP, rows + WB, T), bf16),
            jax.ShapeDtypeStruct((NSRC, T, T), f32),
        ),
        in_specs=[VMEM] * 6,
        out_specs=(VMEM, VMEM, VMEM),
        compiler_params=params(),
    )(recv, features, cotangent, w_self, w_neigh, bias.reshape(1, T))


def segment_of(rows):
    wide = rows.astype(f32)
    return wide[0:WROWS] + wide[WROWS:]


def backward_kernel(dc, entries, totals, tiles, recv, after, out, acc):
    rows = NSRC * T
    parts = group_parts(dc)
    for p in parts:
        for t in range(NSRC):
            acc[t * 16 + p] = jnp.zeros((T, T), f32)

    def group(words):
        sums = []
        for w in words:
            d = dest_of(w) & (NDST - 1)
            row = pl.multiple_of((d & (NSRC - 1)) << 7, T)
            sums.append(
                jnp.dot(recv[d >> 2, pl.ds(row, T), :], tiles[slot_of(w)], preferred_element_type=f32)
            )
        for w, s in zip(words, sums):
            acc[column_of(w)] += s

    walk(entries, dc * CAP, totals[dc], group)
    for j, p in enumerate(parts):
        for t in range(NSRC):
            out[j * rows + t * T : j * rows + (t + 1) * T, :] = acc[t * 16 + p].astype(out.dtype)


def backward(dc, entries, totals, tiles, recv, after):
    rows = NSRC * T
    return pl.pallas_call(
        functools.partial(backward_kernel, dc),
        name=f"backward_{dc}",
        out_shape=jax.ShapeDtypeStruct((8 * rows, T), bf16 if dc else f32),
        in_specs=[SMEM, SMEM, VMEM, VMEM, ANY],
        out_specs=VMEM,
        scratch_shapes=[pltpu.VMEM((80, T, T), f32)],
        compiler_params=params(),
        cost_estimate=pl.CostEstimate(
            flops=4 * 10**9, bytes_accessed=8 * 17 * T * T * 2, transcendentals=0
        ),
    )(entries, totals, tiles, recv, after)


def append(send, seg, seg_got):
    n = send.shape[0]

    def body(send, seg, got, out, alone):
        out[0:n, :] = send[...]
        total = jnp.concatenate(high_low(segment_of(seg[...]) + segment_of(got[...])), axis=0)
        out[n:, :] = total
        alone[...] = total

    shapes = (jax.ShapeDtypeStruct((n + WX, T), bf16), jax.ShapeDtypeStruct((WX, T), bf16))
    return small_call(body, "append", shapes, send, seg, seg_got)


def first_sum(keep, got):
    def body(keep, got, out):
        out[...] = (keep[0 : NSRC * T, :] + got[0 : NSRC * T, :].astype(f32)).astype(bf16)

    return small_call(body, "first_sum", jax.ShapeDtypeStruct((NSRC * T, T), bf16), keep, got)


def core_sums(keep, got, *segs, after):
    rows = NSRC * T
    n = len(segs)

    def body(*refs):
        keep, got, *refs = refs
        segs, (one, three, far, near_two, near, seg) = refs[:n], refs[n:]
        total = segment_of(got[8 * rows :, :])
        for ref in segs:
            total += segment_of(ref[...])
        total = jnp.concatenate(high_low(total), axis=0)
        one[2 * rows :, :] = total
        seg[...] = total
        places = ((one, 0), (three, 0), (far, 0), (near_two, 0), (one, rows), (three, rows), (near, 0))
        for i, (ref, first) in enumerate(places):
            part = slice((i + 1) * rows, (i + 2) * rows)
            value = keep[part, :] + got[part, :].astype(f32)
            ref[first : first + rows, :] = value.astype(ref.dtype)

    def shape(height, kind):
        return jax.ShapeDtypeStruct((height, T), kind)

    shapes = (shape(2 * rows + WX, bf16), shape(2 * rows, bf16))
    shapes += (shape(rows, f32),) * 3 + (shape(WX, bf16),)
    return small_call(body, "core_sums", shapes, keep, got, *segs, after=after)


def rounded_sum(a, b):
    def body(a, b, out):
        out[...] = (a[...] + b[...].astype(f32)).astype(bf16)

    return small_call(body, "rounded_sum", jax.ShapeDtypeStruct(a.shape, bf16), a, b)


def member_segments(spread):
    rows = NSRC * T

    def body(spread, out):
        total = spread[0, rows:, :].astype(f32)
        for m in range(1, REP):
            total += spread[m, rows:, :].astype(f32)
        out[...] = jnp.concatenate(high_low(total[0:WROWS]), axis=0)

    return small_call(body, "member_segments", jax.ShapeDtypeStruct((WX, T), bf16), spread)


def z_sum(near, *parts):
    rows = NSRC * T

    def body(near, a, b, far):
        far[...] = (near[...] + a[0:rows, :].astype(f32) + b[0:rows, :].astype(f32)).astype(bf16)

    return small_call(body, "z_sum", jax.ShapeDtypeStruct((rows, T), bf16), near, *parts)


def z_segments(own, got, after):
    rows = NSRC * T

    def body(own, got, pieces, bias):
        total = segment_of(own[...]) + segment_of(got[2 * rows :, :])
        pieces[...] = total[0:64]
        bias[...] = total[64:]

    shapes = (jax.ShapeDtypeStruct((64, T), f32), jax.ShapeDtypeStruct((WROWS - 64, T), f32))
    return small_call(body, "z_segments", shapes, own, got, after=after)


def final(pieces, bias_rows, near, self_t, far, two, one, three):
    rows = NSRC * T

    def body(p0, p1, p2, p3, bias_rows, near, self_t, far, two, one, three, out, w_self, w_neigh, bias):
        bias[...] = bias_rows[0:1, :]
        for i in range(NSRC):
            part = slice(i * T, (i + 1) * T)
            block = near[part, :] + self_t[i]
            for ref, first in ((far, 0), (two, 0), (one, rows), (three, rows)):
                block += ref[first + i * T : first + (i + 1) * T, :].astype(f32)
            out[part, :] = block.T
        y = lax.axis_index("rep") // 2
        for back, piece in enumerate((p0, p1, p2, p3)):
            to = pl.ds(pl.multiple_of((y - back) % 4 * 32, 32), 32)
            w_self[to, :] = piece[0:32]
            w_neigh[to, :] = piece[32:64]

    shapes = (jax.ShapeDtypeStruct((rows, T), f32),) + (jax.ShapeDtypeStruct((T, T), f32),) * 2
    shapes += (jax.ShapeDtypeStruct((1, T), f32),)
    return small_call(body, "final", shapes, *pieces, bias_rows, near, self_t, far, two, one, three)


def shards(
    features, cotangent, w_self, w_neigh, out_bias, tile_values, dest_tile, src_tile, tile_count
):
    rows = NSRC * T

    two = moved(features, 0, 2, 0)
    pair = glue([(moved(features, 1, 0, 0), 0, rows), (glue([(features, 0, rows)]), 0, rows)])
    one, three = moved(pair, 0, -1, 0), moved(pair, 0, -3, 0)
    far_two = moved(two, 1, 0, 0)
    tiles, deg, entries, totals = load(dest_tile, src_tile, tile_count, tile_values[0, 0], pair)
    held = [(v, 0, rows) for v in (far_two, one, three, pair, two)]
    held += [(v, rows, rows) for v in (one, three, pair)]
    held = glue(held, (deg,))
    acc = forward(0, entries, totals, tiles, held)
    sums = forward(1, entries, totals, tiles, moved(held, 0, 0, 1), acc, deg)
    recv = lax.all_to_all(sums, "rep", 0, 0)

    act, payload, self_t = dense(recv, features, cotangent, w_self, w_neigh, out_bias)
    spread = lax.all_to_all(payload, "rep", 0, 0)

    seg = member_segments(spread)
    seg_got = moved(seg, 1, 0, 0)
    send = backward(1, entries, totals, tiles, spread, seg)
    send, seg = append(send, seg, seg_got)
    keep = backward(0, entries, totals, tiles, spread, seg)
    segs = (seg, moved(seg, 0, 2, 0), moved(seg, 0, 2, 1))
    got = moved(send, 0, 0, 1)
    two = first_sum(keep, got)
    one, three, far, near_two, near, seg = core_sums(keep, got, *segs, after=(two,))
    two = moved(two, 1, 0, 0)
    one, three = moved(one, 0, 1, 0), moved(three, 0, 3, 0)
    two = moved(rounded_sum(near_two, two), 0, 2, 0)
    far = z_sum(far, one, three)
    pieces, bias = z_segments(seg, one, (far,))
    pieces = [pieces] + [moved_y(pieces, dy) for dy in (1, 2, 3)]
    far = moved(far, 1, 0, 0)
    grad_features, grad_w_self, grad_w_neigh, bias = final(pieces, bias, near, self_t, far, two, one, three)
    return (act, grad_features, grad_w_self, grad_w_neigh, bias.reshape(T))


def solution(mesh):
    placed = (
        P(("blk", "rep"), None),
        P(("blk", "rep"), None),
        P(),
        P(),
        P(),
        P("blk", "rep", None, None, None, None),
        P("blk", "rep", None, None),
        P("blk", "rep", None, None),
        P("blk", "rep", None),
    )
    return jax.shard_map(
        shards,
        mesh=mesh,
        in_specs=placed,
        out_specs=(P(("blk", "rep"), None), P(("blk", "rep"), None), P(), P(), P()),
        check_vma=False,
    )
```

```python
import functools

import jax
import jax.numpy as jnp
from jax import lax
from jax.experimental import pallas as pl
from jax.experimental.pallas import tpu as pltpu
from jax.sharding import PartitionSpec as P

f32, bf16 = jnp.float32, jnp.bfloat16
T = 128
SLOTS = 32
NSRC = 4
NDST = 32
REP = 8
CH = 16
STEP_SIZES = (64, 32, 16, 8)
SMALL = STEP_SIZES[-1]
DEG = 16
WROWS = 72
WX = 2 * WROWS
WB = 80
SMEM = pl.BlockSpec(memory_space=pltpu.SMEM)
VMEM = pl.BlockSpec(memory_space=pltpu.VMEM)
ANY = pl.BlockSpec(memory_space=pl.ANY)
HBM = pl.BlockSpec(memory_space=pltpu.HBM)


def params(mib=24):
    return pltpu.CompilerParams(vmem_limit_bytes=mib * 1024 * 1024)


def blk_at(dx, dz, dc):
    here = lax.axis_index("blk")
    x, z, c = here // 8, (here // 2) % 4, here % 2
    return (x + dx) % 2 * 8 + (z + dz) % 4 * 2 + (c + dc) % 2


def moved(value, dx, dz, dc):
    pairs = []
    for i in range(16):
        x, z, c = i // 8, (i // 2) % 4, i % 2
        pairs.append((i, (x + dx) % 2 * 8 + (z + dz) % 4 * 2 + (c + dc) % 2))
    return lax.ppermute(value, "blk", pairs)


def moved_y(value, dy):
    return lax.ppermute(value, "rep", [(i, (i // 2 + dy) % 4 * 2 + i % 2) for i in range(REP)])


def high_low(v):
    high = v.astype(bf16)
    return high, (v - high.astype(f32)).astype(bf16)


def walk(entries, base, count, group):
    def step(first, size):
        group([entries[first + u] for u in range(size)])
        return 0

    end = base + count
    for size in STEP_SIZES:
        steps = (end - base + (size - 1 if size == SMALL else 0)) // size
        lax.fori_loop(0, steps, lambda g, _, base=base, size=size: step(base + g * size, size), 0)
        base = base + steps * size


STEPS = (2, 1, 3, 0)
CAP = 8 * SLOTS + SMALL


def group_parts(dc):
    return [blk_at(dx, dz, dc) for dx in (1, 0) for dz in STEPS]


def slot_of(entry):
    return entry & 511


def column_of(entry):
    return (entry >> 5) & 127


def dest_of(entry):
    return entry >> 12


def make_plan(words, counts, entries, totals):
    none = lax.axis_index("blk") * SLOTS + NSRC * 512 + NDST * 4096
    for dc in range(2):
        end = dc * CAP
        for p in group_parts(dc):

            def put(g, _, p=p, end=end):
                for u in range(8):
                    entries[end + g * 8 + u] = words[0, 0, p, g * 8 + u]
                return 0

            count = counts[0, 0, p]
            lax.fori_loop(0, (count + 7) // 8, put, 0)
            end = end + count
        for u in range(SMALL):
            entries[end + u] = none
        totals[dc] = end - dc * CAP


def load_kernel(
    words_in, counts_in, tiles, after, held, deg_out, entries, totals, acc, sem, words, counts, small_sem
):
    pairs = ((counts_in, counts), (words_in, words))
    small = [pltpu.make_async_copy(a, b, small_sem.at[i]) for i, (a, b) in enumerate(pairs)]
    for copy in small:
        copy.start()
    small[0].wait()

    def each_copy(p, act):
        def go(c, _):
            part = pl.ds(pl.multiple_of(p * SLOTS + c * CH, CH), CH)
            act(pltpu.make_async_copy(tiles.at[p, pl.ds(c * CH, CH)], held.at[part], sem.at[p, c]))
            return 0

        lax.fori_loop(0, (counts[0, 0, p] + CH - 1) // CH, go, 0)

    for p in range(16):
        each_copy(p, lambda copy: copy.start())
    small[1].wait()
    make_plan(words, counts, entries, totals)
    acc[...] = jnp.zeros_like(acc)

    def add(p, _):
        each_copy(p, lambda copy: copy.wait())
        count = counts[0, 0, p]

        def step(g, _):
            for u in range(SMALL):
                k = g * SMALL + u
                d = jnp.where(k < count, dest_of(words[0, 0, p, k]), NDST)
                acc[d] += held[p * SLOTS + k].astype(f32)
            return 0

        lax.fori_loop(0, (count + SMALL - 1) // SMALL, step, 0)
        return 0

    lax.fori_loop(0, 16, add, 0)
    eye = lax.broadcasted_iota(jnp.int32, (T, T), 0) == lax.broadcasted_iota(jnp.int32, (T, T), 1)
    for d in range(NDST):
        column = jnp.sum(acc[d], axis=1, keepdims=True)
        deg_out[d : d + 1, :] = jnp.sum(jnp.where(eye, column, 0.0), axis=0, keepdims=True)


def load(words, tile_count, tiles, after):
    return pl.pallas_call(
        load_kernel,
        name="load",
        out_shape=(
            jax.ShapeDtypeStruct((16 * SLOTS, T, T), bf16),
            jax.ShapeDtypeStruct((NDST, T), f32),
            jax.ShapeDtypeStruct((2 * CAP,), jnp.int32),
            jax.ShapeDtypeStruct((2,), jnp.int32),
        ),
        in_specs=[ANY] * 2 + [HBM, ANY],
        out_specs=(VMEM, VMEM, SMEM, SMEM),
        scratch_shapes=[
            pltpu.VMEM((NDST + 1, T, T), f32),
            pltpu.SemaphoreType.DMA((16, SLOTS // CH)),
            pltpu.SMEM(words.shape, jnp.int32),
            pltpu.SMEM(tile_count.shape, jnp.int32),
            pltpu.SemaphoreType.DMA((2,)),
        ],
        compiler_params=params(),
        cost_estimate=pl.CostEstimate(flops=10**10, bytes_accessed=12 * 10**6, transcendentals=0),
    )(words, tile_count, tiles, after)


def small_call(body, name, shapes, *operands, after=()):
    n = len(operands)
    return pl.pallas_call(
        lambda *refs: body(*refs[:n], *refs[n + len(after) :]),
        name=name,
        out_shape=shapes,
        in_specs=[VMEM] * n + [ANY] * len(after),
        out_specs=VMEM if isinstance(shapes, jax.ShapeDtypeStruct) else (VMEM,) * len(shapes),
        compiler_params=params(8),
    )(*operands, *after)


def stage(features, dest_tile, src_tile, tile_count):
    def body(features, dests, srcs, counts, feat, words, count_out):
        feat[...] = features[...]
        count_out[...] = counts[...]
        shape = dests.shape[2:]
        place = lax.broadcasted_iota(jnp.int32, shape, 0) * SLOTS + lax.broadcasted_iota(jnp.int32, shape, 1)
        words[0, 0] = place + (srcs[0, 0] << 9) + (dests[0, 0] << 12)

    shapes = tuple(jax.ShapeDtypeStruct(v.shape, v.dtype) for v in (features, dest_tile, tile_count))
    return small_call(body, "stage", shapes, features, dest_tile, src_tile, tile_count)


def glue(parts, after=()):
    arrays = []
    for array, _, _ in parts:
        if not any(array is a for a in arrays):
            arrays.append(array)

    def body(*refs):
        *refs, out = refs
        row = 0
        for array, first, rows in parts:
            ref = refs[[array is a for a in arrays].index(True)]
            out[row : row + rows, :] = ref[first : first + rows, :]
            row += rows

    shape = jax.ShapeDtypeStruct((sum(rows for _, _, rows in parts), T), bf16)
    return small_call(body, "glue", shape, *arrays, after=after)


def forward_kernel(dc, entries, totals, tiles, blocks, *refs):
    rows = NSRC * T
    if dc:
        acc_in, deg, out, acc, feat = refs
        acc[0:NDST] = acc_in[0:NDST]
    else:
        acc, feat = refs
        acc[...] = jnp.zeros_like(acc)
    for j, p in enumerate(group_parts(dc)):
        for t in range(NSRC):
            feat[t * 16 + p] = blocks[j * rows + t * T : j * rows + (t + 1) * T, :]

    def group(words):
        sums = [
            jnp.dot(tiles[slot_of(w)], feat[column_of(w)], preferred_element_type=f32) for w in words
        ]
        for w, s in zip(words, sums):
            acc[dest_of(w)] += s

    walk(entries, dc * CAP, totals[dc], group)
    if dc:
        for m in range(REP):
            out[m, 0:rows, :] = acc[m * NSRC : (m + 1) * NSRC].reshape(rows, T).astype(bf16)
            high, low = high_low(deg[m * NSRC : (m + 1) * NSRC, :])
            out[m, rows:, :] = jnp.concatenate(
                [high, low, jnp.zeros((DEG - 2 * NSRC, T), bf16)], axis=0
            )


def forward(dc, entries, totals, tiles, blocks, *extra):
    rows = NSRC * T
    sums = (NDST + 1, T, T)
    if dc:
        shape = jax.ShapeDtypeStruct((REP, rows + DEG, T), bf16)
    else:
        shape = jax.ShapeDtypeStruct(sums, f32)
    return pl.pallas_call(
        functools.partial(forward_kernel, dc),
        name=f"forward_{dc}",
        out_shape=shape,
        in_specs=[SMEM, SMEM] + [VMEM] * (2 + len(extra)),
        out_specs=VMEM,
        scratch_shapes=([pltpu.VMEM(sums, f32)] if dc else []) + [pltpu.VMEM((80, T, T), bf16)],
        compiler_params=params(),
        cost_estimate=pl.CostEstimate(
            flops=4 * 10**9, bytes_accessed=8 * 17 * T * T * 2, transcendentals=0
        ),
    )(entries, totals, tiles, blocks, *extra)


def dense_kernel(recv, features, cotangent, w_self, w_neigh, bias, act, payload, self_t):
    rows = NSRC * T
    total = recv[0, 0:rows, :].astype(f32)
    deg = jnp.zeros((NSRC, T), f32)
    for m in range(REP):
        if m:
            total += recv[m, 0:rows, :].astype(f32)
        extra = recv[m, rows:, :].astype(f32)
        deg += extra[0:NSRC] + extra[NSRC : 2 * NSRC]
    scale = lax.rsqrt(1.0 + deg)
    eye = lax.broadcasted_iota(jnp.int32, (T, T), 0) == lax.broadcasted_iota(jnp.int32, (T, T), 1)
    columns = [
        jnp.sum(jnp.where(eye, scale[i : i + 1, :], 0.0), axis=1, keepdims=True) for i in range(NSRC)
    ]
    mean = (total * jnp.concatenate(columns, axis=0)).astype(bf16)
    feat = features[...]
    pre = (
        jnp.dot(feat, w_self[...], preferred_element_type=f32)
        + jnp.dot(mean, w_neigh[...], preferred_element_type=f32)
        + bias[...]
    )
    sigma = jax.nn.sigmoid(pre)
    act[...] = (pre * sigma).astype(bf16)
    grad = (cotangent[...].astype(f32) * sigma * (1.0 + pre * (1.0 - sigma))).astype(bf16)
    down = (((0,), (0,)), ((), ()))
    across = (((1,), (1,)), ((), ()))
    g_self = lax.dot_general(feat, grad, down, preferred_element_type=f32)
    g_neigh = lax.dot_general(mean, grad, down, preferred_element_type=f32)
    g_bias = jnp.sum(grad.astype(f32), axis=0, keepdims=True)
    sum_t = lax.dot_general(w_neigh[...], grad, across, preferred_element_type=f32)
    own_t = lax.dot_general(w_self[...], grad, across, preferred_element_type=f32)
    spread = []
    for i in range(NSRC):
        part = slice(i * T, (i + 1) * T)
        spread.append((sum_t[:, part] * scale[i : i + 1, :]).astype(bf16))
        self_t[i] = own_t[:, part]
    bias_rows = jnp.broadcast_to(g_bias, (8, T))
    for m in range(REP):
        for i in range(NSRC):
            payload[m, i * T : (i + 1) * T, :] = spread[i]
        piece = slice(m // 2 * 32, (m // 2 + 1) * 32)
        segment = [g_self[piece], g_neigh[piece], bias_rows, jnp.zeros((WB - WROWS, T), f32)]
        payload[m, rows:, :] = jnp.concatenate(segment, axis=0).astype(bf16)


def dense(recv, features, cotangent, w_self, w_neigh, bias):
    rows = NSRC * T
    return pl.pallas_call(
        dense_kernel,
        name="dense",
        out_shape=(
            jax.ShapeDtypeStruct((rows, T), bf16),
            jax.ShapeDtypeStruct((REP, rows + WB, T), bf16),
            jax.ShapeDtypeStruct((NSRC, T, T), f32),
        ),
        in_specs=[VMEM] * 6,
        out_specs=(VMEM, VMEM, VMEM),
        compiler_params=params(),
    )(recv, features, cotangent, w_self, w_neigh, bias.reshape(1, T))


def segment_of(rows):
    wide = rows.astype(f32)
    return wide[0:WROWS] + wide[WROWS:]


def backward_kernel(dc, entries, totals, tiles, recv, after, out, acc):
    rows = NSRC * T
    parts = group_parts(dc)
    for p in parts:
        for t in range(NSRC):
            acc[t * 16 + p] = jnp.zeros((T, T), f32)

    def group(words):
        sums = []
        for w in words:
            d = dest_of(w) & (NDST - 1)
            row = pl.multiple_of((d & (NSRC - 1)) << 7, T)
            sums.append(
                jnp.dot(recv[d >> 2, pl.ds(row, T), :], tiles[slot_of(w)], preferred_element_type=f32)
            )
        for w, s in zip(words, sums):
            acc[column_of(w)] += s

    walk(entries, dc * CAP, totals[dc], group)
    for j, p in enumerate(parts):
        for t in range(NSRC):
            out[j * rows + t * T : j * rows + (t + 1) * T, :] = acc[t * 16 + p].astype(out.dtype)


def backward(dc, entries, totals, tiles, recv, after):
    rows = NSRC * T
    return pl.pallas_call(
        functools.partial(backward_kernel, dc),
        name=f"backward_{dc}",
        out_shape=jax.ShapeDtypeStruct((8 * rows, T), bf16 if dc else f32),
        in_specs=[SMEM, SMEM, VMEM, VMEM, ANY],
        out_specs=VMEM,
        scratch_shapes=[pltpu.VMEM((80, T, T), f32)],
        compiler_params=params(),
        cost_estimate=pl.CostEstimate(
            flops=4 * 10**9, bytes_accessed=8 * 17 * T * T * 2, transcendentals=0
        ),
    )(entries, totals, tiles, recv, after)


def append(send, seg, seg_got):
    n = send.shape[0]

    def body(send, seg, got, out, alone):
        out[0:n, :] = send[...]
        total = jnp.concatenate(high_low(segment_of(seg[...]) + segment_of(got[...])), axis=0)
        out[n:, :] = total
        alone[...] = total

    shapes = (jax.ShapeDtypeStruct((n + WX, T), bf16), jax.ShapeDtypeStruct((WX, T), bf16))
    return small_call(body, "append", shapes, send, seg, seg_got)


def first_sum(keep, got):
    def body(keep, got, out):
        out[...] = (keep[0 : NSRC * T, :] + got[0 : NSRC * T, :].astype(f32)).astype(bf16)

    return small_call(body, "first_sum", jax.ShapeDtypeStruct((NSRC * T, T), bf16), keep, got)


def core_sums(keep, got, *segs, after):
    rows = NSRC * T
    n = len(segs)

    def body(*refs):
        keep, got, *refs = refs
        segs, (one, three, far, near_two, near, seg) = refs[:n], refs[n:]
        total = segment_of(got[8 * rows :, :])
        for ref in segs:
            total += segment_of(ref[...])
        total = jnp.concatenate(high_low(total), axis=0)
        one[2 * rows :, :] = total
        seg[...] = total
        places = ((one, 0), (three, 0), (far, 0), (near_two, 0), (one, rows), (three, rows), (near, 0))
        for i, (ref, first) in enumerate(places):
            part = slice((i + 1) * rows, (i + 2) * rows)
            value = keep[part, :] + got[part, :].astype(f32)
            ref[first : first + rows, :] = value.astype(ref.dtype)

    def shape(height, kind):
        return jax.ShapeDtypeStruct((height, T), kind)

    shapes = (shape(2 * rows + WX, bf16), shape(2 * rows, bf16))
    shapes += (shape(rows, f32),) * 3 + (shape(WX, bf16),)
    return small_call(body, "core_sums", shapes, keep, got, *segs, after=after)


def rounded_sum(a, b):
    def body(a, b, out):
        out[...] = (a[...] + b[...].astype(f32)).astype(bf16)

    return small_call(body, "rounded_sum", jax.ShapeDtypeStruct(a.shape, bf16), a, b)


def member_segments(spread):
    rows = NSRC * T

    def body(spread, out):
        total = spread[0, rows:, :].astype(f32)
        for m in range(1, REP):
            total += spread[m, rows:, :].astype(f32)
        out[...] = jnp.concatenate(high_low(total[0:WROWS]), axis=0)

    return small_call(body, "member_segments", jax.ShapeDtypeStruct((WX, T), bf16), spread)


def z_sum(near, *parts):
    rows = NSRC * T

    def body(near, a, b, far):
        far[...] = (near[...] + a[0:rows, :].astype(f32) + b[0:rows, :].astype(f32)).astype(bf16)

    return small_call(body, "z_sum", jax.ShapeDtypeStruct((rows, T), bf16), near, *parts)


def z_segments(own, got, after):
    rows = NSRC * T

    def body(own, got, pieces, bias):
        total = segment_of(own[...]) + segment_of(got[2 * rows :, :])
        pieces[...] = total[0:64]
        bias[...] = total[64:]

    shapes = (jax.ShapeDtypeStruct((64, T), f32), jax.ShapeDtypeStruct((WROWS - 64, T), f32))
    return small_call(body, "z_segments", shapes, own, got, after=after)


def final(pieces, bias_rows, near, self_t, far, two, one, three):
    rows = NSRC * T

    def body(p0, p1, p2, p3, bias_rows, near, self_t, far, two, one, three, out, w_self, w_neigh, bias):
        bias[...] = bias_rows[0:1, :]
        for i in range(NSRC):
            part = slice(i * T, (i + 1) * T)
            block = near[part, :] + self_t[i]
            for ref, first in ((far, 0), (two, 0), (one, rows), (three, rows)):
                block += ref[first + i * T : first + (i + 1) * T, :].astype(f32)
            out[part, :] = block.T
        y = lax.axis_index("rep") // 2
        for back, piece in enumerate((p0, p1, p2, p3)):
            to = pl.ds(pl.multiple_of((y - back) % 4 * 32, 32), 32)
            w_self[to, :] = piece[0:32]
            w_neigh[to, :] = piece[32:64]

    shapes = (jax.ShapeDtypeStruct((rows, T), f32),) + (jax.ShapeDtypeStruct((T, T), f32),) * 2
    shapes += (jax.ShapeDtypeStruct((1, T), f32),)
    return small_call(body, "final", shapes, *pieces, bias_rows, near, self_t, far, two, one, three)


def shards(
    features, cotangent, w_self, w_neigh, out_bias, tile_values, dest_tile, src_tile, tile_count
):
    rows = NSRC * T

    two = moved(features, 0, 2, 0)
    own, words, counts = stage(features, dest_tile, src_tile, tile_count)
    pair = glue([(moved(features, 1, 0, 0), 0, rows), (own, 0, rows)], (words,))
    one, three = moved(pair, 0, -1, 0), moved(pair, 0, -3, 0)
    far_two = moved(two, 1, 0, 0)
    tiles, deg, entries, totals = load(words, counts, tile_values[0, 0], pair)
    held = [(v, 0, rows) for v in (far_two, one, three, pair, two)]
    held += [(v, rows, rows) for v in (one, three, pair)]
    held = glue(held, (deg,))
    acc = forward(0, entries, totals, tiles, held)
    sums = forward(1, entries, totals, tiles, moved(held, 0, 0, 1), acc, deg)
    recv = lax.all_to_all(sums, "rep", 0, 0)

    act, payload, self_t = dense(recv, features, cotangent, w_self, w_neigh, out_bias)
    spread = lax.all_to_all(payload, "rep", 0, 0)

    seg = member_segments(spread)
    seg_got = moved(seg, 1, 0, 0)
    send = backward(1, entries, totals, tiles, spread, seg)
    send, seg = append(send, seg, seg_got)
    keep = backward(0, entries, totals, tiles, spread, seg)
    segs = (seg, moved(seg, 0, 2, 0), moved(seg, 0, 2, 1))
    got = moved(send, 0, 0, 1)
    two = first_sum(keep, got)
    one, three, far, near_two, near, seg = core_sums(keep, got, *segs, after=(two,))
    two = moved(two, 1, 0, 0)
    one, three = moved(one, 0, 1, 0), moved(three, 0, 3, 0)
    two = moved(rounded_sum(near_two, two), 0, 2, 0)
    far = z_sum(far, one, three)
    pieces, bias = z_segments(seg, one, (far,))
    pieces = [pieces] + [moved_y(pieces, dy) for dy in (1, 2, 3)]
    far = moved(far, 1, 0, 0)
    grad_features, grad_w_self, grad_w_neigh, bias = final(pieces, bias, near, self_t, far, two, one, three)
    return (act, grad_features, grad_w_self, grad_w_neigh, bias.reshape(T))


def solution(mesh):
    placed = (
        P(("blk", "rep"), None),
        P(("blk", "rep"), None),
        P(),
        P(),
        P(),
        P("blk", "rep", None, None, None, None),
        P("blk", "rep", None, None),
        P("blk", "rep", None, None),
        P("blk", "rep", None),
    )
    return jax.shard_map(
        shards,
        mesh=mesh,
        in_specs=placed,
        out_specs=(P(("blk", "rep"), None), P(("blk", "rep"), None), P(), P(), P()),
        check_vma=False,
    )
```

```python
import functools

import jax
import jax.numpy as jnp
from jax import lax
from jax.experimental import pallas as pl
from jax.experimental.pallas import tpu as pltpu
from jax.sharding import PartitionSpec as P

f32, bf16 = jnp.float32, jnp.bfloat16
T = 128
SLOTS = 32
NSRC = 4
NDST = 32
REP = 8
CH = 16
STEP_SIZES = (64, 32, 16, 8)
SMALL = STEP_SIZES[-1]
DEG = 16
WROWS = 72
WX = 2 * WROWS
WB = 80
SMEM = pl.BlockSpec(memory_space=pltpu.SMEM)
VMEM = pl.BlockSpec(memory_space=pltpu.VMEM)
ANY = pl.BlockSpec(memory_space=pl.ANY)
HBM = pl.BlockSpec(memory_space=pltpu.HBM)


def params(mib=24):
    return pltpu.CompilerParams(vmem_limit_bytes=mib * 1024 * 1024)


def blk_at(dx, dz, dc):
    here = lax.axis_index("blk")
    x, z, c = here // 8, (here // 2) % 4, here % 2
    return (x + dx) % 2 * 8 + (z + dz) % 4 * 2 + (c + dc) % 2


def moved(value, dx, dz, dc):
    pairs = []
    for i in range(16):
        x, z, c = i // 8, (i // 2) % 4, i % 2
        pairs.append((i, (x + dx) % 2 * 8 + (z + dz) % 4 * 2 + (c + dc) % 2))
    return lax.ppermute(value, "blk", pairs)


def moved_y(value, dy):
    return lax.ppermute(value, "rep", [(i, (i // 2 + dy) % 4 * 2 + i % 2) for i in range(REP)])


def high_low(v):
    high = v.astype(bf16)
    return high, (v - high.astype(f32)).astype(bf16)


def walk(entries, base, count, group):
    def step(first, size):
        group([entries[first + u] for u in range(size)])
        return 0

    end = base + count
    for size in STEP_SIZES:
        steps = (end - base + (size - 1 if size == SMALL else 0)) // size
        lax.fori_loop(0, steps, lambda g, _, base=base, size=size: step(base + g * size, size), 0)
        base = base + steps * size


STEPS = (2, 1, 3, 0)
CAP = 8 * SLOTS + SMALL


def group_parts(dc):
    return [blk_at(dx, dz, dc) for dx in (1, 0) for dz in STEPS]


def slot_of(entry):
    return entry & 511


def column_of(entry):
    return (entry >> 5) & 127


def dest_of(entry):
    return entry >> 12


def make_plan(words, counts, entries, totals):
    none = lax.axis_index("blk") * SLOTS + NSRC * 512 + NDST * 4096
    for dc in range(2):
        end = dc * CAP
        for p in group_parts(dc):

            def put(g, _, p=p, end=end):
                for u in range(8):
                    entries[end + g * 8 + u] = words[0, 0, p, g * 8 + u]
                return 0

            count = counts[0, 0, p]
            lax.fori_loop(0, (count + 7) // 8, put, 0)
            end = end + count
        for u in range(SMALL):
            entries[end + u] = none
        totals[dc] = end - dc * CAP


def load_kernel(
    words_in, counts_in, tiles, after, held, deg_out, entries, totals, acc, sem, words, counts, small_sem
):
    pairs = ((counts_in, counts), (words_in, words))
    small = [pltpu.make_async_copy(a, b, small_sem.at[i]) for i, (a, b) in enumerate(pairs)]
    for copy in small:
        copy.start()
    small[0].wait()

    def each_copy(p, act):
        def go(c, _):
            part = pl.ds(pl.multiple_of(p * SLOTS + c * CH, CH), CH)
            act(pltpu.make_async_copy(tiles.at[p, pl.ds(c * CH, CH)], held.at[part], sem.at[p, c]))
            return 0

        lax.fori_loop(0, (counts[0, 0, p] + CH - 1) // CH, go, 0)

    for p in range(16):
        each_copy(p, lambda copy: copy.start())
    small[1].wait()
    make_plan(words, counts, entries, totals)
    acc[...] = jnp.zeros_like(acc)

    def add(p, _):
        each_copy(p, lambda copy: copy.wait())
        count = counts[0, 0, p]

        def step(first, size):
            for u in range(size):
                k = first + u
                d = jnp.where(k < count, dest_of(words[0, 0, p, k]), NDST)
                acc[d] += held[p * SLOTS + k].astype(f32)
            return 0

        whole = count // CH
        lax.fori_loop(0, whole, lambda g, _: step(g * CH, CH), 0)
        rest = (count - whole * CH + SMALL - 1) // SMALL
        lax.fori_loop(0, rest, lambda g, _: step(whole * CH + g * SMALL, SMALL), 0)
        return 0

    lax.fori_loop(0, 16, add, 0)
    eye = lax.broadcasted_iota(jnp.int32, (T, T), 0) == lax.broadcasted_iota(jnp.int32, (T, T), 1)
    for d in range(NDST):
        column = jnp.sum(acc[d], axis=1, keepdims=True)
        deg_out[d : d + 1, :] = jnp.sum(jnp.where(eye, column, 0.0), axis=0, keepdims=True)


def load(words, tile_count, tiles, after):
    return pl.pallas_call(
        load_kernel,
        name="load",
        out_shape=(
            jax.ShapeDtypeStruct((16 * SLOTS, T, T), bf16),
            jax.ShapeDtypeStruct((NDST, T), f32),
            jax.ShapeDtypeStruct((2 * CAP,), jnp.int32),
            jax.ShapeDtypeStruct((2,), jnp.int32),
        ),
        in_specs=[ANY] * 2 + [HBM, ANY],
        out_specs=(VMEM, VMEM, SMEM, SMEM),
        scratch_shapes=[
            pltpu.VMEM((NDST + 1, T, T), f32),
            pltpu.SemaphoreType.DMA((16, SLOTS // CH)),
            pltpu.SMEM(words.shape, jnp.int32),
            pltpu.SMEM(tile_count.shape, jnp.int32),
            pltpu.SemaphoreType.DMA((2,)),
        ],
        compiler_params=params(),
        cost_estimate=pl.CostEstimate(flops=10**10, bytes_accessed=12 * 10**6, transcendentals=0),
    )(words, tile_count, tiles, after)


def small_call(body, name, shapes, *operands, after=()):
    n = len(operands)
    return pl.pallas_call(
        lambda *refs: body(*refs[:n], *refs[n + len(after) :]),
        name=name,
        out_shape=shapes,
        in_specs=[VMEM] * n + [ANY] * len(after),
        out_specs=VMEM if isinstance(shapes, jax.ShapeDtypeStruct) else (VMEM,) * len(shapes),
        compiler_params=params(8),
    )(*operands, *after)


def stage(features, dest_tile, src_tile, tile_count):
    def body(features, dests, srcs, counts, feat, words, count_out):
        feat[...] = features[...]
        count_out[...] = counts[...]
        shape = dests.shape[2:]
        place = lax.broadcasted_iota(jnp.int32, shape, 0) * SLOTS + lax.broadcasted_iota(jnp.int32, shape, 1)
        words[0, 0] = place + (srcs[0, 0] << 9) + (dests[0, 0] << 12)

    shapes = tuple(jax.ShapeDtypeStruct(v.shape, v.dtype) for v in (features, dest_tile, tile_count))
    return small_call(body, "stage", shapes, features, dest_tile, src_tile, tile_count)


def glue(parts, after=()):
    arrays = []
    for array, _, _ in parts:
        if not any(array is a for a in arrays):
            arrays.append(array)

    def body(*refs):
        *refs, out = refs
        row = 0
        for array, first, rows in parts:
            ref = refs[[array is a for a in arrays].index(True)]
            out[row : row + rows, :] = ref[first : first + rows, :]
            row += rows

    shape = jax.ShapeDtypeStruct((sum(rows for _, _, rows in parts), T), bf16)
    return small_call(body, "glue", shape, *arrays, after=after)


def forward_kernel(dc, entries, totals, tiles, blocks, *refs):
    rows = NSRC * T
    if dc:
        acc_in, deg, out, acc, feat = refs
        acc[0:NDST] = acc_in[0:NDST]
    else:
        acc, feat = refs
        acc[...] = jnp.zeros_like(acc)
    for j, p in enumerate(group_parts(dc)):
        for t in range(NSRC):
            feat[t * 16 + p] = blocks[j * rows + t * T : j * rows + (t + 1) * T, :]

    def group(words):
        sums = [
            jnp.dot(tiles[slot_of(w)], feat[column_of(w)], preferred_element_type=f32) for w in words
        ]
        for w, s in zip(words, sums):
            acc[dest_of(w)] += s

    walk(entries, dc * CAP, totals[dc], group)
    if dc:
        for m in range(REP):
            out[m, 0:rows, :] = acc[m * NSRC : (m + 1) * NSRC].reshape(rows, T).astype(bf16)
            high, low = high_low(deg[m * NSRC : (m + 1) * NSRC, :])
            out[m, rows:, :] = jnp.concatenate(
                [high, low, jnp.zeros((DEG - 2 * NSRC, T), bf16)], axis=0
            )


def forward(dc, entries, totals, tiles, blocks, *extra):
    rows = NSRC * T
    sums = (NDST + 1, T, T)
    if dc:
        shape = jax.ShapeDtypeStruct((REP, rows + DEG, T), bf16)
    else:
        shape = jax.ShapeDtypeStruct(sums, f32)
    return pl.pallas_call(
        functools.partial(forward_kernel, dc),
        name=f"forward_{dc}",
        out_shape=shape,
        in_specs=[SMEM, SMEM] + [VMEM] * (2 + len(extra)),
        out_specs=VMEM,
        scratch_shapes=([pltpu.VMEM(sums, f32)] if dc else []) + [pltpu.VMEM((80, T, T), bf16)],
        compiler_params=params(),
        cost_estimate=pl.CostEstimate(
            flops=4 * 10**9, bytes_accessed=8 * 17 * T * T * 2, transcendentals=0
        ),
    )(entries, totals, tiles, blocks, *extra)


def dense_kernel(recv, features, cotangent, w_self, w_neigh, bias, act, payload, self_t):
    rows = NSRC * T
    total = recv[0, 0:rows, :].astype(f32)
    deg = jnp.zeros((NSRC, T), f32)
    for m in range(REP):
        if m:
            total += recv[m, 0:rows, :].astype(f32)
        extra = recv[m, rows:, :].astype(f32)
        deg += extra[0:NSRC] + extra[NSRC : 2 * NSRC]
    scale = lax.rsqrt(1.0 + deg)
    eye = lax.broadcasted_iota(jnp.int32, (T, T), 0) == lax.broadcasted_iota(jnp.int32, (T, T), 1)
    columns = [
        jnp.sum(jnp.where(eye, scale[i : i + 1, :], 0.0), axis=1, keepdims=True) for i in range(NSRC)
    ]
    mean = (total * jnp.concatenate(columns, axis=0)).astype(bf16)
    feat = features[...]
    pre = (
        jnp.dot(feat, w_self[...], preferred_element_type=f32)
        + jnp.dot(mean, w_neigh[...], preferred_element_type=f32)
        + bias[...]
    )
    sigma = jax.nn.sigmoid(pre)
    act[...] = (pre * sigma).astype(bf16)
    grad = (cotangent[...].astype(f32) * sigma * (1.0 + pre * (1.0 - sigma))).astype(bf16)
    down = (((0,), (0,)), ((), ()))
    across = (((1,), (1,)), ((), ()))
    g_self = lax.dot_general(feat, grad, down, preferred_element_type=f32)
    g_neigh = lax.dot_general(mean, grad, down, preferred_element_type=f32)
    g_bias = jnp.sum(grad.astype(f32), axis=0, keepdims=True)
    sum_t = lax.dot_general(w_neigh[...], grad, across, preferred_element_type=f32)
    own_t = lax.dot_general(w_self[...], grad, across, preferred_element_type=f32)
    spread = []
    for i in range(NSRC):
        part = slice(i * T, (i + 1) * T)
        spread.append((sum_t[:, part] * scale[i : i + 1, :]).astype(bf16))
        self_t[i] = own_t[:, part]
    bias_rows = jnp.broadcast_to(g_bias, (8, T))
    for m in range(REP):
        for i in range(NSRC):
            payload[m, i * T : (i + 1) * T, :] = spread[i]
        piece = slice(m // 2 * 32, (m // 2 + 1) * 32)
        segment = [g_self[piece], g_neigh[piece], bias_rows, jnp.zeros((WB - WROWS, T), f32)]
        payload[m, rows:, :] = jnp.concatenate(segment, axis=0).astype(bf16)


def dense(recv, features, cotangent, w_self, w_neigh, bias):
    rows = NSRC * T
    return pl.pallas_call(
        dense_kernel,
        name="dense",
        out_shape=(
            jax.ShapeDtypeStruct((rows, T), bf16),
            jax.ShapeDtypeStruct((REP, rows + WB, T), bf16),
            jax.ShapeDtypeStruct((NSRC, T, T), f32),
        ),
        in_specs=[VMEM] * 6,
        out_specs=(VMEM, VMEM, VMEM),
        compiler_params=params(),
    )(recv, features, cotangent, w_self, w_neigh, bias.reshape(1, T))


def segment_of(rows):
    wide = rows.astype(f32)
    return wide[0:WROWS] + wide[WROWS:]


def backward_kernel(dc, entries, totals, tiles, recv, after, out, acc):
    rows = NSRC * T
    parts = group_parts(dc)
    for p in parts:
        for t in range(NSRC):
            acc[t * 16 + p] = jnp.zeros((T, T), f32)

    def group(words):
        sums = []
        for w in words:
            d = dest_of(w) & (NDST - 1)
            row = pl.multiple_of((d & (NSRC - 1)) << 7, T)
            sums.append(
                jnp.dot(recv[d >> 2, pl.ds(row, T), :], tiles[slot_of(w)], preferred_element_type=f32)
            )
        for w, s in zip(words, sums):
            acc[column_of(w)] += s

    walk(entries, dc * CAP, totals[dc], group)
    for j, p in enumerate(parts):
        for t in range(NSRC):
            out[j * rows + t * T : j * rows + (t + 1) * T, :] = acc[t * 16 + p].astype(out.dtype)


def backward(dc, entries, totals, tiles, recv, after):
    rows = NSRC * T
    return pl.pallas_call(
        functools.partial(backward_kernel, dc),
        name=f"backward_{dc}",
        out_shape=jax.ShapeDtypeStruct((8 * rows, T), bf16 if dc else f32),
        in_specs=[SMEM, SMEM, VMEM, VMEM, ANY],
        out_specs=VMEM,
        scratch_shapes=[pltpu.VMEM((80, T, T), f32)],
        compiler_params=params(),
        cost_estimate=pl.CostEstimate(
            flops=4 * 10**9, bytes_accessed=8 * 17 * T * T * 2, transcendentals=0
        ),
    )(entries, totals, tiles, recv, after)


def append(send, seg, seg_got):
    n = send.shape[0]

    def body(send, seg, got, out, alone):
        out[0:n, :] = send[...]
        total = jnp.concatenate(high_low(segment_of(seg[...]) + segment_of(got[...])), axis=0)
        out[n:, :] = total
        alone[...] = total

    shapes = (jax.ShapeDtypeStruct((n + WX, T), bf16), jax.ShapeDtypeStruct((WX, T), bf16))
    return small_call(body, "append", shapes, send, seg, seg_got)


def first_sum(keep, got):
    def body(keep, got, out):
        out[...] = (keep[0 : NSRC * T, :] + got[0 : NSRC * T, :].astype(f32)).astype(bf16)

    return small_call(body, "first_sum", jax.ShapeDtypeStruct((NSRC * T, T), bf16), keep, got)


def core_sums(keep, got, *segs, after):
    rows = NSRC * T
    n = len(segs)

    def body(*refs):
        keep, got, *refs = refs
        segs, (one, three, far, near_two, near, seg) = refs[:n], refs[n:]
        total = segment_of(got[8 * rows :, :])
        for ref in segs:
            total += segment_of(ref[...])
        total = jnp.concatenate(high_low(total), axis=0)
        one[2 * rows :, :] = total
        seg[...] = total
        places = ((one, 0), (three, 0), (far, 0), (near_two, 0), (one, rows), (three, rows), (near, 0))
        for i, (ref, first) in enumerate(places):
            part = slice((i + 1) * rows, (i + 2) * rows)
            value = keep[part, :] + got[part, :].astype(f32)
            ref[first : first + rows, :] = value.astype(ref.dtype)

    def shape(height, kind):
        return jax.ShapeDtypeStruct((height, T), kind)

    shapes = (shape(2 * rows + WX, bf16), shape(2 * rows, bf16))
    shapes += (shape(rows, f32),) * 3 + (shape(WX, bf16),)
    return small_call(body, "core_sums", shapes, keep, got, *segs, after=after)


def rounded_sum(a, b):
    def body(a, b, out):
        out[...] = (a[...] + b[...].astype(f32)).astype(bf16)

    return small_call(body, "rounded_sum", jax.ShapeDtypeStruct(a.shape, bf16), a, b)


def member_segments(spread):
    rows = NSRC * T

    def body(spread, out):
        total = spread[0, rows:, :].astype(f32)
        for m in range(1, REP):
            total += spread[m, rows:, :].astype(f32)
        out[...] = jnp.concatenate(high_low(total[0:WROWS]), axis=0)

    return small_call(body, "member_segments", jax.ShapeDtypeStruct((WX, T), bf16), spread)


def z_sum(near, *parts):
    rows = NSRC * T

    def body(near, a, b, far):
        far[...] = (near[...] + a[0:rows, :].astype(f32) + b[0:rows, :].astype(f32)).astype(bf16)

    return small_call(body, "z_sum", jax.ShapeDtypeStruct((rows, T), bf16), near, *parts)


def z_segments(own, got, after):
    rows = NSRC * T

    def body(own, got, pieces, bias):
        total = segment_of(own[...]) + segment_of(got[2 * rows :, :])
        pieces[...] = total[0:64]
        bias[...] = total[64:]

    shapes = (jax.ShapeDtypeStruct((64, T), f32), jax.ShapeDtypeStruct((WROWS - 64, T), f32))
    return small_call(body, "z_segments", shapes, own, got, after=after)


def final(pieces, bias_rows, near, self_t, far, two, one, three):
    rows = NSRC * T

    def body(p0, p1, p2, p3, bias_rows, near, self_t, far, two, one, three, out, w_self, w_neigh, bias):
        bias[...] = bias_rows[0:1, :]
        for i in range(NSRC):
            part = slice(i * T, (i + 1) * T)
            block = near[part, :] + self_t[i]
            for ref, first in ((far, 0), (two, 0), (one, rows), (three, rows)):
                block += ref[first + i * T : first + (i + 1) * T, :].astype(f32)
            out[part, :] = block.T
        y = lax.axis_index("rep") // 2
        for back, piece in enumerate((p0, p1, p2, p3)):
            to = pl.ds(pl.multiple_of((y - back) % 4 * 32, 32), 32)
            w_self[to, :] = piece[0:32]
            w_neigh[to, :] = piece[32:64]

    shapes = (jax.ShapeDtypeStruct((rows, T), f32),) + (jax.ShapeDtypeStruct((T, T), f32),) * 2
    shapes += (jax.ShapeDtypeStruct((1, T), f32),)
    return small_call(body, "final", shapes, *pieces, bias_rows, near, self_t, far, two, one, three)


def shards(
    features, cotangent, w_self, w_neigh, out_bias, tile_values, dest_tile, src_tile, tile_count
):
    rows = NSRC * T

    two = moved(features, 0, 2, 0)
    own, words, counts = stage(features, dest_tile, src_tile, tile_count)
    pair = glue([(moved(features, 1, 0, 0), 0, rows), (own, 0, rows)], (words,))
    one, three = moved(pair, 0, -1, 0), moved(pair, 0, -3, 0)
    far_two = moved(two, 1, 0, 0)
    tiles, deg, entries, totals = load(words, counts, tile_values[0, 0], pair)
    held = [(v, 0, rows) for v in (far_two, one, three, pair, two)]
    held += [(v, rows, rows) for v in (one, three, pair)]
    held = glue(held, (deg,))
    acc = forward(0, entries, totals, tiles, held)
    sums = forward(1, entries, totals, tiles, moved(held, 0, 0, 1), acc, deg)
    recv = lax.all_to_all(sums, "rep", 0, 0)

    act, payload, self_t = dense(recv, features, cotangent, w_self, w_neigh, out_bias)
    spread = lax.all_to_all(payload, "rep", 0, 0)

    seg = member_segments(spread)
    seg_got = moved(seg, 1, 0, 0)
    send = backward(1, entries, totals, tiles, spread, seg)
    send, seg = append(send, seg, seg_got)
    keep = backward(0, entries, totals, tiles, spread, seg)
    segs = (seg, moved(seg, 0, 2, 0), moved(seg, 0, 2, 1))
    got = moved(send, 0, 0, 1)
    two = first_sum(keep, got)
    one, three, far, near_two, near, seg = core_sums(keep, got, *segs, after=(two,))
    two = moved(two, 1, 0, 0)
    one, three = moved(one, 0, 1, 0), moved(three, 0, 3, 0)
    two = moved(rounded_sum(near_two, two), 0, 2, 0)
    far = z_sum(far, one, three)
    pieces, bias = z_segments(seg, one, (far,))
    pieces = [pieces] + [moved_y(pieces, dy) for dy in (1, 2, 3)]
    far = moved(far, 1, 0, 0)
    grad_features, grad_w_self, grad_w_neigh, bias = final(pieces, bias, near, self_t, far, two, one, three)
    return (act, grad_features, grad_w_self, grad_w_neigh, bias.reshape(T))


def solution(mesh):
    placed = (
        P(("blk", "rep"), None),
        P(("blk", "rep"), None),
        P(),
        P(),
        P(),
        P("blk", "rep", None, None, None, None),
        P("blk", "rep", None, None),
        P("blk", "rep", None, None),
        P("blk", "rep", None),
    )
    return jax.shard_map(
        shards,
        mesh=mesh,
        in_specs=placed,
        out_specs=(P(("blk", "rep"), None), P(("blk", "rep"), None), P(), P(), P()),
        check_vma=False,
    )
```
